512 devices in a mesh: dp: 4 (over x), expert: 128 (over y, z, core).
Axes of the slice: x: 4, y: 8, z: 8, core: 2. Of those that a mesh axis runs over, the one named last changes fastest.
Arguments:
- tokens: bfloat16 [16384, 1024], P(('dp', 'expert')), may hold values from -6 to 6
- cotangent: bfloat16 [16384, 1024], P(('dp', 'expert')), may hold values from -3 to 3
- routes: int32 [16384, 8], P(('dp', 'expert')), may hold values from 0 to 127, as said below
- combine: bfloat16 [16384, 8], P(('dp', 'expert')), may hold values from 0.099609375 to 1
- hot_experts: int32 [4], replicated, may hold values from 0 to 63, as said below
- extra_slots: int32 [4], replicated, may hold values from 1 to 2, as said below
- w_gate: bfloat16 [128, 1024, 384], P('expert'), may hold values from -0.1875 to 0.1875
- w_up: bfloat16 [128, 1024, 384], P('expert'), may hold values from -0.1875 to 0.1875
- w_down: bfloat16 [128, 384, 1024], P('expert'), may hold values from -0.3125 to 0.3125
Outputs:
- token_grads: bfloat16 [16384, 1024], P(('dp', 'expert'))
- grad_gate: bfloat16 [128, 1024, 384], P('expert', 'dp')
- grad_up: bfloat16 [128, 1024, 384], P('expert', 'dp')
- grad_down: bfloat16 [128, 384, 1024], P('expert')
The draws below stay inside these ranges and needn't reach their ends.
Inputs may be any that keep to these rules, and one draw needn't show every extreme that they name: `routes`: each row names 8 different experts. `hot_experts`: 4 different experts, all below 64. `extra_slots`: one of the entries equals 2.
All inputs are finite; a program needn't handle non-finite values.
Results may differ from the reference program's by a relative error of at most 0.0064.
Values may be sent and summed in bfloat16 or wider, within the bound.
No kernel may reach another device: no remote copies, remote signals or barrier semaphores. Data moves between devices by JAX's collectives and lax.ppermute only.
A program may use at most 64 MiB of HBM per device.

```python
import jax
import jax.numpy as jnp
from jax import lax

D = 1024
HID = 384
TOP = 8
HOT = 4
TOK_DEV = 32
SPECIALIST_COUNT = 128
TOKENS = 16384
CAP = 2
EXTRA = 2


def route_tables(key):
    base_key = jax.random.fold_in(key, 4242)
    subkeys = jax.random.split(base_key, 7)
    middle_list = 1 + jax.random.permutation(subkeys[0], SPECIALIST_COUNT // 2 - 2)[:HOT - 2]
    ends_list = jnp.array([SPECIALIST_COUNT // 2 - 1, 0], dtype=jnp.int32)
    joined_list = jnp.concatenate([ends_list, middle_list.astype(jnp.int32)])
    hot_list = jax.random.permutation(subkeys[6], joined_list).astype(jnp.int32)
    extra_list = jax.random.randint(subkeys[1], (HOT,), 1, EXTRA + 1, dtype=jnp.int32)
    full_slot = jax.random.randint(subkeys[2], (), 0, HOT, dtype=jnp.int32)
    hot_order = jnp.arange(HOT, dtype=jnp.int32)
    extra_list = jnp.where(hot_order == full_slot, EXTRA, extra_list).astype(jnp.int32)
    specialist_saturated = jnp.sum(jnp.where(hot_order == full_slot, hot_list, 0))
    block_count = TOKENS // TOK_DEV
    block_keys = jax.random.split(subkeys[3], block_count)

    def block_order(block_key):
        return jax.random.permutation(block_key, TOK_DEV)
    position = jax.vmap(block_order)(block_keys).reshape(-1)
    mandated_assignment_choice = position < CAP + EXTRA
    specialist_dimension = jnp.arange(SPECIALIST_COUNT, dtype=jnp.int32)
    enrolled_marker = jnp.any(specialist_dimension[None, :] == hot_list[:, None], axis=0)
    stochastic_tosses = jax.random.randint(subkeys[4], (TOKENS, SPECIALIST_COUNT), 0, 2, dtype=jnp.int32)
    stochastic_jitter = jax.random.randint(subkeys[5], (TOKENS, SPECIALIST_COUNT), 0, 65536, dtype=jnp.int32)
    logit_increment = jnp.where(enrolled_marker[None, :], stochastic_tosses, 0)
    logit_increment = logit_increment + jnp.where((specialist_dimension[None, :] == specialist_saturated) & mandated_assignment_choice[:, None], 2, 0)
    gating_logits = (stochastic_jitter + logit_increment * 65536) * SPECIALIST_COUNT + specialist_dimension[None, :]
    chosen = lax.top_k(gating_logits, TOP)[1].astype(jnp.int32)
    return (hot_list, extra_list, chosen)


def draw_routes(key, part):
    return route_tables(key)[2]


def draw_hot_experts(key, part):
    return route_tables(key)[0]


def draw_extra_slots(key, part):
    return route_tables(key)[1]


def level_of(own_key, shape, pieces, smallest, top_value):
    loudness = 1.0
    for dim, parts in pieces:
        draws = jax.random.uniform(jax.random.fold_in(jax.random.fold_in(own_key, 6), dim), (parts,), jnp.float32, smallest / len(pieces), top_value / len(pieces))
        loudness = loudness * jnp.repeat(jnp.exp(draws), shape[dim] // parts).reshape((-1,) + (1,) * (len(shape) - 1 - dim))
    return loudness


def bell_draw(own_key, shape, spread, reach, cuts=(), kind=jnp.bfloat16):
    values = jax.random.normal(own_key, shape, jnp.float32) * spread
    if len(cuts) > 0:
        values = level_of(own_key, shape, cuts, -0.22, 0.18) * values
    return jnp.clip(values, min=-reach, max=reach).astype(kind)


def setup_inputs(seed: int = 0) -> dict:
    splits = jax.random.split(jax.random.key(seed), 10)
    tokens = bell_draw(splits[0], (TOKENS, D), 1.0, 6.0, ((0, 512),))
    cotangent = bell_draw(splits[1], (TOKENS, D), 0.5, 3.0, ((0, 512),))
    routes = draw_routes(jax.random.fold_in(splits[9], 71), 0)
    combine = jnp.clip(0.099609375 + 0.9003906 * jax.random.uniform(splits[3], (TOKENS, TOP), jnp.float32) ** level_of(splits[3], (TOKENS, TOP), ((0, 512),), -0.2, 0.2), 0.099609375, 1.0).astype(jnp.bfloat16)
    hot_experts = draw_hot_experts(jax.random.fold_in(splits[9], 71), 0)
    extra_slots = draw_extra_slots(jax.random.fold_in(splits[9], 71), 0)
    w_gate = bell_draw(splits[6], (SPECIALIST_COUNT, D, HID), D ** -0.5, 0.1875, ((0, 128),))
    w_up = bell_draw(splits[7], (SPECIALIST_COUNT, D, HID), D ** -0.5, 0.1875, ((0, 128),))
    w_down = bell_draw(splits[8], (SPECIALIST_COUNT, HID, D), HID ** -0.5, 0.3125, ((0, 128),))
    return dict(tokens=tokens, cotangent=cotangent, routes=routes, combine=combine, hot_experts=hot_experts, extra_slots=extra_slots, w_gate=w_gate, w_up=w_up, w_down=w_down)


def expert_pass(weight_gate, weight_up, weight_down, row_tokens, row_cotan, row_weights):
    gate_pre = jnp.dot(row_tokens, weight_gate, preferred_element_type=jnp.float32)
    up_proj = jnp.dot(row_tokens, weight_up, preferred_element_type=jnp.float32)
    sigmoid_gate = jax.nn.sigmoid(gate_pre)
    gate_act = gate_pre * sigmoid_gate
    hidden = (gate_act * up_proj).astype(jnp.bfloat16)
    out_grad = (row_weights.astype(jnp.float32)[:, None] * row_cotan.astype(jnp.float32)).astype(jnp.bfloat16)
    grad_down = jnp.dot(hidden.T, out_grad, preferred_element_type=jnp.float32)
    hidden_grad = jnp.dot(out_grad, weight_down.T, preferred_element_type=jnp.float32)
    gate_grad = (hidden_grad * up_proj * sigmoid_gate * (1.0 + gate_pre * (1.0 - sigmoid_gate))).astype(jnp.bfloat16)
    up_grad = (hidden_grad * gate_act).astype(jnp.bfloat16)
    grad_gate = jnp.dot(row_tokens.T, gate_grad, preferred_element_type=jnp.float32)
    grad_up = jnp.dot(row_tokens.T, up_grad, preferred_element_type=jnp.float32)
    row_grads = jnp.dot(gate_grad, weight_gate.T, preferred_element_type=jnp.float32)
    row_grads = row_grads + jnp.dot(up_grad, weight_up.T, preferred_element_type=jnp.float32)
    return row_grads.astype(jnp.bfloat16), (grad_gate, grad_up, grad_down)


def reference(tokens, cotangent, routes, combine, hot_experts, extra_slots, w_gate, w_up, w_down):
    block_count = TOKENS // TOK_DEV
    assign_count = TOK_DEV * TOP
    expert_ids = routes.reshape(block_count, assign_count)
    assign_order = jnp.arange(assign_count, dtype=jnp.int32)

    def rank_block(block_ids):
        earlier = (block_ids[:, None] == block_ids[None, :]) & (assign_order[None, :] < assign_order[:, None])
        return jnp.sum(earlier.astype(jnp.int32), axis=1)

    slot_rank = lax.map(rank_block, expert_ids)
    hot_match = expert_ids[:, :, None] == hot_experts[None, None, :]
    slot_limit = CAP + jnp.sum(jnp.where(hot_match, extra_slots[None, None, :], 0), axis=2)
    is_kept = slot_rank < slot_limit
    block_index = jnp.broadcast_to(jnp.arange(block_count, dtype=jnp.int32)[:, None], (block_count, assign_count))
    global_index = block_index * assign_count + assign_order[None, :]
    base_expert = jnp.where(slot_rank < CAP, expert_ids, SPECIALIST_COUNT)
    base_table = jnp.full((SPECIALIST_COUNT, block_count, CAP), -1, jnp.int32)
    base_table = base_table.at[base_expert, block_index, jnp.minimum(slot_rank, CAP - 1)].set(global_index, mode="drop")
    spill_kept = is_kept & (slot_rank >= CAP)
    spill_expert = jnp.where(spill_kept, expert_ids, SPECIALIST_COUNT)
    spill_table = jnp.full((SPECIALIST_COUNT, block_count, EXTRA), -1, jnp.int32)
    spill_table = spill_table.at[spill_expert, block_index, jnp.clip(slot_rank - CAP, 0, EXTRA - 1)].set(global_index, mode="drop")
    enrolled_marker = jnp.any(jnp.arange(SPECIALIST_COUNT, dtype=jnp.int32)[:, None] == hot_experts[None, :], axis=1)
    combine_flat = combine.reshape(-1)

    def rows_pass(weight_gate, weight_up, weight_down, table, accum):
        flat_table = table.reshape(-1)
        valid = flat_table >= 0
        safe_index = jnp.where(valid, flat_table, 0)
        token_index = safe_index // TOP
        row_weights = jnp.where(valid, combine_flat[safe_index], jnp.zeros((), combine.dtype))
        row_grads, grad_terms = expert_pass(weight_gate, weight_up, weight_down, tokens[token_index], cotangent[token_index], row_weights)
        accum = accum.at[token_index].add(row_grads.astype(jnp.float32))
        return accum, grad_terms

    def per_expert(accum, expert):
        weight_gate = w_gate[expert]
        weight_up = w_up[expert]
        weight_down = w_down[expert]
        accum, base_terms = rows_pass(weight_gate, weight_up, weight_down, base_table[expert], accum)

        def with_spill(current):
            return rows_pass(weight_gate, weight_up, weight_down, spill_table[expert], current)

        def without_spill(current):
            empty_gate = jnp.zeros((D, HID), jnp.float32)
            return current, (empty_gate, empty_gate, jnp.zeros((HID, D), jnp.float32))

        accum, spill_terms = lax.cond(enrolled_marker[expert], with_spill, without_spill, accum)
        totals = (
            (base_terms[0] + spill_terms[0]).astype(jnp.bfloat16),
            (base_terms[1] + spill_terms[1]).astype(jnp.bfloat16),
            (base_terms[2] + spill_terms[2]).astype(jnp.bfloat16),
        )
        return accum, totals

    accum, stacked = lax.scan(per_expert, jnp.zeros((TOKENS, D), jnp.float32), jnp.arange(SPECIALIST_COUNT, dtype=jnp.int32))
    return accum.astype(jnp.bfloat16), stacked[0], stacked[1], stacked[2]
```

```python
import functools

import jax
import jax.numpy as jnp
from jax import lax
from jax.experimental import pallas as pl
from jax.experimental.pallas import tpu as pltpu
from jax.sharding import PartitionSpec as P

BASE = 2
SLOTS = 4
MSG = 2 * SLOTS
LANES = 128
F32 = jnp.float32
BF16 = jnp.bfloat16
VMEM = pl.BlockSpec(memory_space=pltpu.VMEM)
SMEM = pl.BlockSpec(memory_space=pltpu.SMEM)
VMEM_BYTES = 48 * 1024 * 1024


def call(body, name, out_shape, in_specs, scratch=(), flops=0, bytes_accessed=0):
    return pl.pallas_call(
        body,
        name=name,
        out_shape=out_shape,
        in_specs=in_specs,
        out_specs=jax.tree.map(lambda _: VMEM, out_shape),
        scratch_shapes=list(scratch),
        compiler_params=pltpu.CompilerParams(vmem_limit_bytes=VMEM_BYTES),
        cost_estimate=pl.CostEstimate(
            flops=flops, bytes_accessed=bytes_accessed, transcendentals=0
        ),
    )


def dispatch_body(experts, routes, combine, hot, extra, tok, cot, send, pick, both):
    count, width = tok.shape
    both[:count, :] = tok[...]
    both[count:, :] = cot[...]
    lanes = 2 * count
    expert_id = lax.broadcasted_iota(jnp.int32, (experts, lanes), 0)
    lane = lax.broadcasted_iota(jnp.int32, (experts, lanes), 1)
    named = jnp.zeros((experts, lanes), F32)
    weight = jnp.zeros((experts, lanes), F32)
    for k in range(routes.shape[0]):
        match = expert_id == routes[k : k + 1, :]
        named = named + jnp.where(match, 1.0, 0.0)
        weight = weight + jnp.where(match, combine[k : k + 1, :], 0.0)
    src = lax.broadcasted_iota(jnp.int32, (lanes, lanes), 0)
    dst = lax.broadcasted_iota(jnp.int32, (lanes, lanes), 1)
    dst = jnp.where(dst >= count, dst - count, dst)
    before = jnp.where(src < dst, 1.0, 0.0)
    before = jnp.where(src < count, before, 0.0).astype(BF16)
    rank = jnp.dot(named.astype(BF16), before, preferred_element_type=F32)
    limit = jnp.full((experts, lanes), float(BASE), F32)
    for j in range(hot.shape[0]):
        limit = limit + jnp.where(expert_id == hot[j], extra[j].astype(F32), 0.0)
    place = jnp.where(lane >= count, rank + float(SLOTS), rank)
    place = jnp.where(named > 0.5, place, -1.0)
    place = jnp.where(rank < limit, place, -1.0)
    weight = jnp.where(lane >= count, weight, 1.0)
    slot = lax.broadcasted_iota(jnp.int32, (experts, MSG, lanes), 1).astype(F32)
    hit = jnp.broadcast_to(place[:, None, :], (experts, MSG, lanes)) == slot
    scaled = jnp.where(hit, jnp.broadcast_to(weight[:, None, :], hit.shape), 0.0)
    pick[...] = jnp.where(hit, 1.0, 0.0).reshape(experts * MSG, lanes).astype(BF16)
    scaled = scaled.reshape(experts * MSG, lanes).astype(BF16)
    send[...] = jnp.dot(scaled, both[...], preferred_element_type=F32).astype(BF16)


NN = (((1,), (0,)), ((), ()))
NT = (((1,), (1,)), ((), ()))
TN = (((0,), (0,)), ((), ()))


def dot(a, b, dims):
    return lax.dot_general(a, b, dims, preferred_element_type=F32)


def rows_body(recv, w_gate, w_up, w_down, back, tok, og, gu, hid, wide, narrow):
    total, features = recv.shape
    peers = total // MSG
    hidden = w_gate.shape[1]
    half = features // 2
    for c in range(features // LANES):
        wide[c] = recv[:, c * LANES : (c + 1) * LANES].astype(F32)
    for part in range(2):
        first = part * (SLOTS // 2)
        rows = pl.ds(first * peers, 2 * peers)
        for s in range(2):
            at = pl.ds((first + s) * peers, peers)
            for c in range(features // LANES):
                cols = slice(c * LANES, (c + 1) * LANES)
                tok[at, cols] = wide[c, pl.ds(first + s, peers, MSG), :].astype(BF16)
                og[at, cols] = wide[c, pl.ds(first + s + SLOTS, peers, MSG), :].astype(BF16)
        x, g = tok[rows, :], og[rows, :]
        gate_pre = dot(x, w_gate[...], NN)
        up_proj = dot(x, w_up[...], NN)
        hidden_grad = dot(g, w_down[...], NT)
        s = jax.nn.sigmoid(gate_pre)
        act = gate_pre * s
        hid[rows, :] = (act * up_proj).astype(BF16)
        gate_grad = (hidden_grad * up_proj * s * (1.0 + gate_pre * (1.0 - s))).astype(BF16)
        up_grad = (hidden_grad * act).astype(BF16)
        gu[rows, :hidden] = gate_grad
        gu[rows, hidden:] = up_grad
        grads = dot(gate_grad, w_gate[...], NT) + dot(up_grad, w_up[...], NT)
        for s in range(2):
            piece = grads[s * peers : (s + 1) * peers, :]
            for c in range(half // LANES):
                low = piece[:, c * LANES : (c + 1) * LANES]
                high = piece[:, half + c * LANES : half + (c + 1) * LANES]
                narrow[c, pl.ds(first + s, peers, MSG), :] = low
                narrow[c, pl.ds(first + s + SLOTS, peers, MSG), :] = high
    for c in range(half // LANES):
        back[:, c * LANES : (c + 1) * LANES] = narrow[c].astype(BF16)


def weights_body(ranks, me, left, right, own, *rest):
    sends, total = rest[:-1], rest[-1]
    total[...] = dot(left[...], right[...], TN)
    piece = own.shape[0]
    own[...] = total[pl.ds(pl.multiple_of(me[0] * piece, 8), piece), :]
    for i in range(1, ranks):
        at = lax.rem(me[0] + i, ranks) * piece
        sends[i - 1][...] = total[pl.ds(pl.multiple_of(at, 8), piece), :].astype(BF16)


def weight_pieces(name, ranks, me, left, right):
    rows, depth, width = left.shape[0], left.shape[1], right.shape[1]
    piece = depth // ranks
    out = [jax.ShapeDtypeStruct((piece, width), F32)]
    out += [jax.ShapeDtypeStruct((piece, width), BF16)] * (ranks - 1)
    return call(
        functools.partial(weights_body, ranks),
        name,
        out,
        [SMEM, VMEM, VMEM],
        [pltpu.VMEM((depth, width), F32)],
        2 * rows * depth * width,
        2 * (rows * (depth + width) + 2 * depth * width),
    )(me, left, right)


def sum_over(axis, ranks, pieces):
    total = pieces[0]
    for i in range(1, ranks):
        total = total + lax.ppermute(
            pieces[i], axis, [(s, (s + i) % ranks) for s in range(ranks)]
        ).astype(F32)
    return total.astype(BF16)


def shards(tokens, cotangent, routes, combine, hot_experts, extra_slots, w_gate, w_up, w_down):
    experts = lax.axis_size("expert")
    ranks = lax.axis_size("dp")
    count, features = tokens.shape
    hidden = w_gate.shape[2]
    total = experts * MSG
    rows = experts * SLOTS
    route_lanes = jnp.concatenate([routes, routes], axis=0).T
    combine_lanes = jnp.concatenate([combine, combine], axis=0).astype(F32).T
    send, pick = call(
        functools.partial(dispatch_body, experts),
        "dispatch",
        [
            jax.ShapeDtypeStruct((total, features), BF16),
            jax.ShapeDtypeStruct((total, 2 * count), BF16),
        ],
        [VMEM, VMEM, SMEM, SMEM, VMEM, VMEM],
        [pltpu.VMEM((2 * count, features), BF16)],
        2 * total * 2 * count * features,
        2 * total * features,
    )(route_lanes, combine_lanes, hot_experts, extra_slots, tokens, cotangent)
    recv = lax.all_to_all(send, "expert", split_axis=0, concat_axis=0, tiled=True)
    back, tok, og, gu, hid = call(
        rows_body,
        "rows",
        [
            jax.ShapeDtypeStruct((total, features // 2), BF16),
            jax.ShapeDtypeStruct((rows, features), BF16),
            jax.ShapeDtypeStruct((rows, features), BF16),
            jax.ShapeDtypeStruct((rows, 2 * hidden), BF16),
            jax.ShapeDtypeStruct((rows, hidden), BF16),
        ],
        [VMEM] * 4,
        [
            pltpu.VMEM((features // LANES, total, LANES), F32),
            pltpu.VMEM((features // 2 // LANES, total, LANES), F32),
        ],
        10 * rows * features * hidden,
        2 * (total * features * 2 + 3 * features * hidden),
    )(recv, w_gate[0], w_up[0], w_down[0])
    returned = lax.all_to_all(back, "expert", split_axis=0, concat_axis=0, tiled=True)
    me = lax.axis_index("dp").astype(jnp.int32).reshape(1)
    down = sum_over("dp", ranks, weight_pieces("down_grad", ranks, me, hid, og))
    grad_down = lax.all_gather(down, "dp", axis=0, tiled=True)
    gate_up = sum_over("dp", ranks, weight_pieces("gate_up_grad", ranks, me, tok, gu))
    halves = dot(pick, returned, TN)
    token_grads = jnp.concatenate([halves[:count], halves[count:]], axis=1).astype(BF16)
    return (
        token_grads,
        gate_up[None, :, :hidden],
        gate_up[None, :, hidden:],
        grad_down[None],
    )


def solution(mesh):
    in_specs = (
        P(("dp", "expert"), None),
        P(("dp", "expert"), None),
        P(("dp", "expert"), None),
        P(("dp", "expert"), None),
        P(),
        P(),
        P("expert", None, None),
        P("expert", None, None),
        P("expert", None, None),
    )
    out_specs = (
        P(("dp", "expert"), None),
        P("expert", "dp", None),
        P("expert", "dp", None),
        P("expert", None, None),
    )
    return jax.shard_map(shards, mesh=mesh, in_specs=in_specs, out_specs=out_specs, check_vma=False)
```

```python
import functools

import jax
import jax.numpy as jnp
from jax import lax
from jax.experimental import pallas as pl
from jax.experimental.pallas import tpu as pltpu
from jax.sharding import PartitionSpec as P

BASE = 2
SLOTS = 4
MSG = 2 * SLOTS
LANES = 128
F32 = jnp.float32
BF16 = jnp.bfloat16
VMEM = pl.BlockSpec(memory_space=pltpu.VMEM)
SMEM = pl.BlockSpec(memory_space=pltpu.SMEM)
MIB = 1024 * 1024


NN = (((1,), (0,)), ((), ()))
NT = (((1,), (1,)), ((), ()))
TN = (((0,), (0,)), ((), ()))


def dot(a, b, dims):
    return lax.dot_general(a, b, dims, preferred_element_type=F32)


def call(
    body, name, out_shape, in_specs, scratch=(), flops=0, bytes_accessed=0, vmem=16 * MIB
):
    return pl.pallas_call(
        body,
        name=name,
        out_shape=out_shape,
        in_specs=in_specs,
        out_specs=jax.tree.map(lambda _: VMEM, out_shape),
        scratch_shapes=list(scratch),
        compiler_params=pltpu.CompilerParams(vmem_limit_bytes=vmem),
        cost_estimate=pl.CostEstimate(
            flops=flops, bytes_accessed=bytes_accessed, transcendentals=0
        ),
    )


def identity(n):
    rows = lax.broadcasted_iota(jnp.int32, (n, n), 0)
    return jnp.where(rows == lax.broadcasted_iota(jnp.int32, (n, n), 1), 1.0, 0.0).astype(BF16)


def dispatch_body(
    experts, tok_hbm, cot_hbm, routes_hbm, combine_hbm, hot_hbm, extra_hbm,
    send, pick_t, both, routes_in, combine_in, hot, extra, sems,
):
    count = tok_hbm.shape[0]
    copies = [
        pltpu.make_async_copy(source, target, sems.at[i])
        for i, (source, target) in enumerate(
            [
                (routes_hbm, routes_in),
                (combine_hbm, combine_in),
                (hot_hbm, hot),
                (extra_hbm, extra),
                (tok_hbm, both.at[pl.ds(0, count)]),
                (cot_hbm, both.at[pl.ds(count, count)]),
            ]
        )
    ]
    for copy in copies:
        copy.start()
    for copy in copies[:4]:
        copy.wait()
    lanes = 2 * count
    src = lax.broadcasted_iota(jnp.int32, (count, lanes), 0)
    dst = lax.broadcasted_iota(jnp.int32, (count, lanes), 1)
    dst = jnp.where(dst >= count, dst - count, dst)
    twice = jnp.where(src == dst, 1.0, 0.0).astype(BF16)
    routes = dot(routes_in[...].astype(F32).astype(BF16), twice, NN)
    combine = dot(combine_in[...], twice, NN)
    expert_id = lax.broadcasted_iota(jnp.int32, (experts, lanes), 0)
    lane = lax.broadcasted_iota(jnp.int32, (experts, lanes), 1)
    named = jnp.zeros((experts, lanes), F32)
    weight = jnp.zeros((experts, lanes), F32)
    expert_number = expert_id.astype(F32)
    for k in range(routes.shape[0]):
        match = expert_number == routes[k : k + 1, :]
        named = named + jnp.where(match, 1.0, 0.0)
        weight = weight + jnp.where(match, combine[k : k + 1, :], 0.0)
    before = jnp.where(src < dst, 1.0, 0.0).astype(BF16)
    rank = dot(named[:, :count].astype(BF16), before, NN)
    limit = jnp.full((experts, lanes), float(BASE), F32)
    for j in range(hot.shape[0]):
        limit = limit + jnp.where(expert_id == hot[j], extra[j].astype(F32), 0.0)
    place = jnp.where(lane >= count, rank + float(SLOTS), rank)
    place = jnp.where(named > 0.5, place, -1.0)
    place = jnp.where(rank < limit, place, -1.0)
    weight = jnp.where(lane >= count, weight, 1.0)
    slot = lax.broadcasted_iota(jnp.int32, (experts, MSG, lanes), 1).astype(F32)
    hit = jnp.broadcast_to(place[:, None, :], (experts, MSG, lanes)) == slot
    scaled = jnp.where(hit, jnp.broadcast_to(weight[:, None, :], hit.shape), 0.0)
    scaled = scaled.reshape(experts * MSG, lanes).astype(BF16)
    for copy in copies[4:]:
        copy.wait()
    send[...] = jnp.dot(scaled, both[...], preferred_element_type=F32).astype(BF16)
    pick = jnp.where(hit, 1.0, 0.0).reshape(experts * MSG, lanes).astype(BF16)
    pick_t[...] = dot(identity(lanes), pick, NT).astype(BF16)


def token_body(pick_t, returned, out):
    count, half = out.shape[0], returned.shape[1]
    both = dot(pick_t[...], returned[...], NN)
    out[:, :half] = both[:count].astype(BF16)
    out[:, half:] = both[count:].astype(BF16)


def place_body(ranks, me, *refs):
    pieces, out = refs[:-1], refs[-1]
    piece = pieces[0].shape[0]
    for i in range(ranks):
        at = lax.rem(me[0] + ranks - i, ranks) * piece
        out[pl.ds(pl.multiple_of(at, 16), piece), :] = pieces[i][...]


def rows_body(recv, w_gate, w_up, w_down, back, tok, og, gu, hid, wide, narrow):
    total, features = recv.shape
    peers = total // MSG
    hidden = w_gate.shape[1]
    half = features // 2
    for c in range(features // LANES):
        wide[c] = recv[:, c * LANES : (c + 1) * LANES].astype(F32)
    for part in range(2):
        first = part * (SLOTS // 2)
        rows = pl.ds(first * peers, 2 * peers)
        for s in range(2):
            at = pl.ds((first + s) * peers, peers)
            for c in range(features // LANES):
                cols = slice(c * LANES, (c + 1) * LANES)
                tok[at, cols] = wide[c, pl.ds(first + s, peers, MSG), :].astype(BF16)
                og[at, cols] = wide[c, pl.ds(first + s + SLOTS, peers, MSG), :].astype(BF16)
        x, g = tok[rows, :], og[rows, :]
        gate_pre = dot(x, w_gate[...], NN)
        up_proj = dot(x, w_up[...], NN)
        hidden_grad = dot(g, w_down[...], NT)
        s = jax.nn.sigmoid(gate_pre)
        act = gate_pre * s
        hid[rows, :] = (act * up_proj).astype(BF16)
        gate_grad = (hidden_grad * up_proj * s * (1.0 + gate_pre * (1.0 - s))).astype(BF16)
        up_grad = (hidden_grad * act).astype(BF16)
        gu[rows, :hidden] = gate_grad
        gu[rows, hidden:] = up_grad
        grads = dot(gate_grad, w_gate[...], NT) + dot(up_grad, w_up[...], NT)
        for s in range(2):
            piece = grads[s * peers : (s + 1) * peers, :]
            for c in range(half // LANES):
                low = piece[:, c * LANES : (c + 1) * LANES]
                high = piece[:, half + c * LANES : half + (c + 1) * LANES]
                narrow[c, pl.ds(first + s, peers, MSG), :] = low
                narrow[c, pl.ds(first + s + SLOTS, peers, MSG), :] = high
    for c in range(half // LANES):
        back[:, c * LANES : (c + 1) * LANES] = narrow[c].astype(BF16)


def weights_body(ranks, me, left, right, own, *rest):
    sends, total = rest[:-1], rest[-1]
    total[...] = dot(left[...], right[...], TN)
    piece = own.shape[0]
    own[...] = total[pl.ds(pl.multiple_of(me[0] * piece, 8), piece), :]
    for i in range(1, ranks):
        at = lax.rem(me[0] + i, ranks) * piece
        sends[i - 1][...] = total[pl.ds(pl.multiple_of(at, 8), piece), :].astype(BF16)


def weight_pieces(name, ranks, me, left, right):
    rows, depth, width = left.shape[0], left.shape[1], right.shape[1]
    piece = depth // ranks
    out = [jax.ShapeDtypeStruct((piece, width), F32)]
    out += [jax.ShapeDtypeStruct((piece, width), BF16)] * (ranks - 1)
    return call(
        functools.partial(weights_body, ranks),
        name,
        out,
        [SMEM, VMEM, VMEM],
        [pltpu.VMEM((depth, width), F32)],
        2 * rows * depth * width,
        2 * (rows * (depth + width) + 2 * depth * width),
    )(me, left, right)


def shift(value, ranks, by):
    return lax.ppermute(value, "dp", [(s, (s + by) % ranks) for s in range(ranks)])


def sum_over(ranks, pieces):
    total = pieces[0]
    for i in range(1, ranks):
        total = total + shift(pieces[i], ranks, i).astype(F32)
    return total.astype(BF16)


def shards(tokens, cotangent, routes, combine, hot_experts, extra_slots, w_gate, w_up, w_down):
    experts = lax.axis_size("expert")
    ranks = lax.axis_size("dp")
    count, features = tokens.shape
    hidden = w_gate.shape[2]
    total = experts * MSG
    rows = experts * SLOTS
    send, pick_t = call(
        functools.partial(dispatch_body, experts),
        "dispatch",
        [
            jax.ShapeDtypeStruct((total, features), BF16),
            jax.ShapeDtypeStruct((2 * count, total), BF16),
        ],
        [pl.BlockSpec(memory_space=pltpu.HBM)] * 6,
        [
            pltpu.VMEM((2 * count, features), BF16),
            pltpu.VMEM(routes.shape[::-1], jnp.int32),
            pltpu.VMEM(combine.shape[::-1], BF16),
            pltpu.SMEM(hot_experts.shape, jnp.int32),
            pltpu.SMEM(extra_slots.shape, jnp.int32),
            pltpu.SemaphoreType.DMA((6,)),
        ],
        2 * total * 2 * count * features,
        2 * total * features,
        64 * MIB - 65536,
    )(tokens, cotangent, routes.T, combine.T, hot_experts, extra_slots)
    recv = lax.all_to_all(send, "expert", split_axis=0, concat_axis=0, tiled=True)
    back, tok, og, gu, hid = call(
        rows_body,
        "rows",
        [
            jax.ShapeDtypeStruct((total, features // 2), BF16),
            jax.ShapeDtypeStruct((rows, features), BF16),
            jax.ShapeDtypeStruct((rows, features), BF16),
            jax.ShapeDtypeStruct((rows, 2 * hidden), BF16),
            jax.ShapeDtypeStruct((rows, hidden), BF16),
        ],
        [VMEM] * 4,
        [
            pltpu.VMEM((features // LANES, total, LANES), F32),
            pltpu.VMEM((features // 2 // LANES, total, LANES), F32),
        ],
        10 * rows * features * hidden,
        2 * (total * features * 2 + 3 * features * hidden),
        32 * MIB,
    )(recv, w_gate[0], w_up[0], w_down[0])
    returned = lax.all_to_all(back, "expert", split_axis=0, concat_axis=0, tiled=True)
    me = lax.axis_index("dp").astype(jnp.int32).reshape(1)
    down = sum_over(ranks, weight_pieces("down_grad", ranks, me, hid, og))
    grad_down = call(
        functools.partial(place_body, ranks),
        "place",
        jax.ShapeDtypeStruct((hidden, features), BF16),
        [SMEM] + [VMEM] * ranks,
        (),
        0,
        4 * hidden * features,
    )(me, down, *(shift(down, ranks, i) for i in range(1, ranks)))
    gate_up = sum_over(ranks, weight_pieces("gate_up_grad", ranks, me, tok, gu))
    token_grads = call(
        token_body,
        "token_grad",
        jax.ShapeDtypeStruct((count, features), BF16),
        [VMEM, VMEM],
        (),
        2 * total * count * features,
        2 * total * features,
    )(pick_t, returned)
    return (
        token_grads,
        gate_up[None, :, :hidden],
        gate_up[None, :, hidden:],
        grad_down[None],
    )


def solution(mesh):
    in_specs = (
        P(("dp", "expert"), None),
        P(("dp", "expert"), None),
        P(("dp", "expert"), None),
        P(("dp", "expert"), None),
        P(),
        P(),
        P("expert", None, None),
        P("expert", None, None),
        P("expert", None, None),
    )
    out_specs = (
        P(("dp", "expert"), None),
        P("expert", "dp", None),
        P("expert", "dp", None),
        P("expert", None, None),
    )
    return jax.shard_map(shards, mesh=mesh, in_specs=in_specs, out_specs=out_specs, check_vma=False)
```

```python
import functools

import jax
import jax.numpy as jnp
from jax import lax
from jax.experimental import pallas as pl
from jax.experimental.pallas import tpu as pltpu
from jax.sharding import PartitionSpec as P

BASE = 2
SLOTS = 4
MSG = 2 * SLOTS
LANES = 128
CHUNKS = 4
F32 = jnp.float32
BF16 = jnp.bfloat16
VMEM = pl.BlockSpec(memory_space=pltpu.VMEM)
ANY = pl.BlockSpec(memory_space=pl.ANY)
SMEM = pl.BlockSpec(memory_space=pltpu.SMEM)
MIB = 1024 * 1024


NN = (((1,), (0,)), ((), ()))
NT = (((1,), (1,)), ((), ()))
TN = (((0,), (0,)), ((), ()))


def dot(a, b, dims):
    return lax.dot_general(a, b, dims, preferred_element_type=F32)


def call(
    body, name, out_shape, in_specs, scratch=(), flops=0, bytes_accessed=0, vmem=16 * MIB, out=VMEM
):
    return pl.pallas_call(
        body,
        name=name,
        out_shape=out_shape,
        in_specs=in_specs,
        out_specs=jax.tree.map(lambda _: out, out_shape),
        scratch_shapes=list(scratch),
        compiler_params=pltpu.CompilerParams(vmem_limit_bytes=vmem),
        cost_estimate=pl.CostEstimate(
            flops=flops, bytes_accessed=bytes_accessed, transcendentals=0
        ),
    )


def identity(n):
    rows = lax.broadcasted_iota(jnp.int32, (n, n), 0)
    return jnp.where(rows == lax.broadcasted_iota(jnp.int32, (n, n), 1), 1.0, 0.0).astype(BF16)


def dispatch_body(
    experts, tok_hbm, cot_hbm, routes_hbm, combine_hbm, hot_hbm, extra_hbm,
    send, pick_t, both, routes_in, combine_in, hot, extra, sems,
):
    count = tok_hbm.shape[0]
    copies = [
        pltpu.make_async_copy(source, target, sems.at[i])
        for i, (source, target) in enumerate(
            [
                (routes_hbm, routes_in),
                (combine_hbm, combine_in),
                (hot_hbm, hot),
                (extra_hbm, extra),
                (tok_hbm, both.at[pl.ds(0, count)]),
                (cot_hbm, both.at[pl.ds(count, count)]),
            ]
        )
    ]
    for copy in copies:
        copy.start()
    for copy in copies[:4]:
        copy.wait()
    lanes = 2 * count
    src = lax.broadcasted_iota(jnp.int32, (count, lanes), 0)
    dst = lax.broadcasted_iota(jnp.int32, (count, lanes), 1)
    dst = jnp.where(dst >= count, dst - count, dst)
    twice = jnp.where(src == dst, 1.0, 0.0).astype(BF16)
    routes = dot(routes_in[...].astype(F32).astype(BF16), twice, NN)
    combine = dot(combine_in[...], twice, NN)
    expert_id = lax.broadcasted_iota(jnp.int32, (experts, lanes), 0)
    lane = lax.broadcasted_iota(jnp.int32, (experts, lanes), 1)
    named = jnp.zeros((experts, lanes), F32)
    weight = jnp.zeros((experts, lanes), F32)
    expert_number = expert_id.astype(F32)
    for k in range(routes.shape[0]):
        match = expert_number == routes[k : k + 1, :]
        named = named + jnp.where(match, 1.0, 0.0)
        weight = weight + jnp.where(match, combine[k : k + 1, :], 0.0)
    before = jnp.where(src < dst, 1.0, 0.0).astype(BF16)
    rank = dot(named[:, :count].astype(BF16), before, NN)
    limit = jnp.full((experts, lanes), float(BASE), F32)
    for j in range(hot.shape[0]):
        limit = limit + jnp.where(expert_id == hot[j], extra[j].astype(F32), 0.0)
    place = jnp.where(lane >= count, rank + float(SLOTS), rank)
    place = jnp.where(named > 0.5, place, -1.0)
    place = jnp.where(rank < limit, place, -1.0)
    weight = jnp.where(lane >= count, weight, 1.0)
    slot = lax.broadcasted_iota(jnp.int32, (experts, MSG, lanes), 1).astype(F32)
    hit = jnp.broadcast_to(place[:, None, :], (experts, MSG, lanes)) == slot
    scaled = jnp.where(hit, jnp.broadcast_to(weight[:, None, :], hit.shape), 0.0)
    scaled = scaled.reshape(experts * MSG, lanes).astype(BF16)
    for copy in copies[4:]:
        copy.wait()
    send[...] = jnp.dot(scaled, both[...], preferred_element_type=F32).astype(BF16)
    pick = jnp.where(hit, 1.0, 0.0).reshape(experts * MSG, lanes).astype(BF16)
    pick_t[...] = dot(identity(lanes), pick, NT).astype(BF16)


def token_body(pick_t, returned, out):
    count, half = out.shape[0], returned.shape[1]
    both = dot(pick_t[...], returned[...], NN)
    out[:, :half] = both[:count].astype(BF16)
    out[:, half:] = both[count:].astype(BF16)


def expert_body(
    ranks, me, recv_hbm, w_gate_hbm, w_up_hbm, w_down_hbm,
    back_hbm, down_a_hbm, down_b_hbm, gate_send_hbm, up_send_hbm, gate_keep_hbm, up_keep_hbm,
    recv, w_gate, w_up, w_down,
    back, down_a, down_b, gate_send, up_send, gate_keep, up_keep,
    wide, narrow, tok, og, gate_rows, up_rows, hid, total, in_sems, out_sems,
):
    rows_in, features = recv.shape
    peers = rows_in // MSG
    half = features // 2
    step = rows_in // CHUNKS
    arrivals = []
    for n in range(CHUNKS):
        at = pl.ds(n * step, step)
        arrivals.append(pltpu.make_async_copy(recv_hbm.at[at], recv.at[at], in_sems.at[n]))
    for n, (source, target) in enumerate(
        [(w_gate_hbm, w_gate), (w_up_hbm, w_up), (w_down_hbm, w_down)]
    ):
        arrivals.append(pltpu.make_async_copy(source, target, in_sems.at[CHUNKS + n]))
    for copy in arrivals:
        copy.start()
    departures = []

    def send_out(source, target):
        copy = pltpu.make_async_copy(source, target, out_sems.at[len(departures)])
        copy.start()
        departures.append(copy)

    for n in range(CHUNKS):
        arrivals[n].wait()
        at = pl.ds(n * step, step)
        for c in range(features // LANES):
            wide[c, at, :] = recv[at, c * LANES : (c + 1) * LANES].astype(F32)
    for copy in arrivals[CHUNKS:]:
        copy.wait()
    for part in range(2):
        first = part * (SLOTS // 2)
        rows = pl.ds(first * peers, 2 * peers)
        for s in range(2):
            at = pl.ds((first + s) * peers, peers)
            for c in range(features // LANES):
                cols = slice(c * LANES, (c + 1) * LANES)
                tok[at, cols] = wide[c, pl.ds(first + s, peers, MSG), :].astype(BF16)
                og[at, cols] = wide[c, pl.ds(first + s + SLOTS, peers, MSG), :].astype(BF16)
        x, g = tok[rows, :], og[rows, :]
        gate_pre = dot(x, w_gate[...], NN)
        up_proj = dot(x, w_up[...], NN)
        hidden_grad = dot(g, w_down[...], NT)
        s = jax.nn.sigmoid(gate_pre)
        act = gate_pre * s
        hid[rows, :] = (act * up_proj).astype(BF16)
        gate_grad = (hidden_grad * up_proj * s * (1.0 + gate_pre * (1.0 - s))).astype(BF16)
        up_grad = (hidden_grad * act).astype(BF16)
        gate_rows[rows, :] = gate_grad
        up_rows[rows, :] = up_grad
        grads = dot(gate_grad, w_gate[...], NT) + dot(up_grad, w_up[...], NT)
        for s in range(2):
            piece = grads[s * peers : (s + 1) * peers, :]
            for c in range(half // LANES):
                low = piece[:, c * LANES : (c + 1) * LANES]
                high = piece[:, half + c * LANES : half + (c + 1) * LANES]
                narrow[c, pl.ds(first + s, peers, MSG), :] = low
                narrow[c, pl.ds(first + s + SLOTS, peers, MSG), :] = high
    for c in range(half // LANES):
        back[:, c * LANES : (c + 1) * LANES] = narrow[c].astype(BF16)
    send_out(back, back_hbm)
    piece = gate_keep.shape[0] // 2
    even = me[0] + 1 - 2 * lax.rem(me[0], 2)
    mirror = ranks - 1 - me[0]
    opposite = ranks - 1 - even

    def part_of(index):
        return total[pl.ds(pl.multiple_of(index * piece, 16), piece), :]

    for grads, keep, send, keep_hbm, send_hbm, near, far in (
        (gate_rows, gate_keep, gate_send, gate_keep_hbm, gate_send_hbm, even, mirror),
        (up_rows, up_keep, up_send, up_keep_hbm, up_send_hbm, mirror, even),
    ):
        total[...] = dot(tok[...], grads[...], TN)
        keep[:piece, :] = part_of(me[0])
        keep[piece:, :] = part_of(near)
        send_out(keep, keep_hbm)
        send[:piece, :] = part_of(far).astype(BF16)
        send[piece:, :] = part_of(opposite).astype(BF16)
        send_out(send, send_hbm)
    down = dot(hid[...], og[...], TN)
    cut = down_a.shape[0]
    down_a[...] = down[:cut].astype(BF16)
    send_out(down_a, down_a_hbm)
    down_b[...] = down[cut:].astype(BF16)
    send_out(down_b, down_b_hbm)
    for copy in departures:
        copy.wait()


def add(kept, received):
    return kept.astype(F32) + received.astype(F32)


def shards(tokens, cotangent, routes, combine, hot_experts, extra_slots, w_gate, w_up, w_down):
    experts = lax.axis_size("expert")
    ranks = lax.axis_size("dp")
    count, features = tokens.shape
    hidden = w_gate.shape[2]
    total = experts * MSG
    rows = experts * SLOTS
    send, pick_t = call(
        functools.partial(dispatch_body, experts),
        "dispatch",
        [
            jax.ShapeDtypeStruct((total, features), BF16),
            jax.ShapeDtypeStruct((2 * count, total), BF16),
        ],
        [ANY] * 6,
        [
            pltpu.VMEM((2 * count, features), BF16),
            pltpu.VMEM(routes.shape[::-1], jnp.int32),
            pltpu.VMEM(combine.shape[::-1], BF16),
            pltpu.SMEM(hot_experts.shape, jnp.int32),
            pltpu.SMEM(extra_slots.shape, jnp.int32),
            pltpu.SemaphoreType.DMA((6,)),
        ],
        2 * total * 2 * count * features,
        2 * total * features,
        64 * MIB - 65536,
    )(tokens, cotangent, routes.T, combine.T, hot_experts, extra_slots)
    recv = lax.all_to_all(send, "expert", split_axis=0, concat_axis=0, tiled=True)
    me = lax.axis_index("dp").astype(jnp.int32).reshape(1)
    piece = features // ranks
    cut = hidden // 2
    pieces = [
        jax.ShapeDtypeStruct((total, features // 2), BF16),
        jax.ShapeDtypeStruct((cut, features), BF16),
        jax.ShapeDtypeStruct((cut, features), BF16),
        jax.ShapeDtypeStruct((2 * piece, hidden), BF16),
        jax.ShapeDtypeStruct((2 * piece, hidden), BF16),
        jax.ShapeDtypeStruct((2 * piece, hidden), F32),
        jax.ShapeDtypeStruct((2 * piece, hidden), F32),
    ]
    operands = (recv, w_gate[0], w_up[0], w_down[0])
    back, down_a, down_b, gate_send, up_send, gate_keep, up_keep = call(
        functools.partial(expert_body, ranks),
        "expert",
        pieces,
        [SMEM] + [ANY] * 4,
        [pltpu.VMEM(a.shape, a.dtype) for a in operands]
        + [pltpu.VMEM(a.shape, a.dtype) for a in pieces]
        + [
            pltpu.VMEM((features // LANES, total, LANES), F32),
            pltpu.VMEM((features // 2 // LANES, total, LANES), F32),
            pltpu.VMEM((rows, features), BF16),
            pltpu.VMEM((rows, features), BF16),
            pltpu.VMEM((rows, hidden), BF16),
            pltpu.VMEM((rows, hidden), BF16),
            pltpu.VMEM((rows, hidden), BF16),
            pltpu.VMEM((features, hidden), F32),
            pltpu.SemaphoreType.DMA((CHUNKS + 3,)),
            pltpu.SemaphoreType.DMA((len(pieces),)),
        ],
        16 * rows * features * hidden,
        2 * (total * features * 2 + 6 * features * hidden),
        64 * MIB - 65536,
        ANY,
    )(me, *operands)
    returned = lax.all_to_all(back, "expert", split_axis=0, concat_axis=0, tiled=True)

    def even(value):
        return lax.ppermute(value, "dp", [(i, i ^ 1) for i in range(ranks)])

    def mirror(value):
        return lax.ppermute(value, "dp", [(i, ranks - 1 - i) for i in range(ranks)])

    sum_a = add(down_a, even(down_a)).astype(BF16)
    sum_b = add(down_b, mirror(down_b)).astype(BF16)
    gate_in, up_in = mirror(gate_send), even(up_send)
    down = jnp.concatenate([add(sum_a, mirror(sum_a)), add(sum_b, even(sum_b))], axis=0)
    gate_next = even(add(gate_keep[piece:], gate_in[piece:]).astype(BF16))
    up_next = mirror(add(up_keep[piece:], up_in[piece:]).astype(BF16))
    grad_gate = add(add(gate_keep[:piece], gate_in[:piece]), gate_next)
    grad_up = add(add(up_keep[:piece], up_in[:piece]), up_next)
    token_grads = call(
        token_body,
        "token_grad",
        jax.ShapeDtypeStruct((count, features), BF16),
        [VMEM, VMEM],
        (),
        2 * total * count * features,
        2 * total * features,
    )(pick_t, returned)
    return (
        token_grads,
        grad_gate[None].astype(BF16),
        grad_up[None].astype(BF16),
        down[None].astype(BF16),
    )


def solution(mesh):
    in_specs = (
        P(("dp", "expert"), None),
        P(("dp", "expert"), None),
        P(("dp", "expert"), None),
        P(("dp", "expert"), None),
        P(),
        P(),
        P("expert", None, None),
        P("expert", None, None),
        P("expert", None, None),
    )
    out_specs = (
        P(("dp", "expert"), None),
        P("expert", "dp", None),
        P("expert", "dp", None),
        P("expert", None, None),
    )
    return jax.shard_map(shards, mesh=mesh, in_specs=in_specs, out_specs=out_specs, check_vma=False)
```

```python
import functools

import jax
import jax.numpy as jnp
from jax import lax
from jax.experimental import pallas as pl
from jax.experimental.pallas import tpu as pltpu
from jax.sharding import PartitionSpec as P

BASE = 2
SLOTS = 4
MSG = 2 * SLOTS
LANES = 128
CHUNKS = 4
F32 = jnp.float32
BF16 = jnp.bfloat16
VMEM = pl.BlockSpec(memory_space=pltpu.VMEM)
ANY = pl.BlockSpec(memory_space=pl.ANY)
SMEM = pl.BlockSpec(memory_space=pltpu.SMEM)
MIB = 1024 * 1024


NN = (((1,), (0,)), ((), ()))
NT = (((1,), (1,)), ((), ()))
TN = (((0,), (0,)), ((), ()))


def dot(a, b, dims):
    return lax.dot_general(a, b, dims, preferred_element_type=F32)


def call(
    body, name, out_shape, in_specs, scratch=(), flops=0, bytes_accessed=0, vmem=16 * MIB, out=VMEM
):
    return pl.pallas_call(
        body,
        name=name,
        out_shape=out_shape,
        in_specs=in_specs,
        out_specs=jax.tree.map(lambda _: out, out_shape),
        scratch_shapes=list(scratch),
        compiler_params=pltpu.CompilerParams(vmem_limit_bytes=vmem),
        cost_estimate=pl.CostEstimate(
            flops=flops, bytes_accessed=bytes_accessed, transcendentals=0
        ),
    )


def identity(n):
    rows = lax.broadcasted_iota(jnp.int32, (n, n), 0)
    return jnp.where(rows == lax.broadcasted_iota(jnp.int32, (n, n), 1), 1.0, 0.0).astype(BF16)


def dispatch_body(
    experts, tok_hbm, cot_hbm, routes_hbm, combine_hbm, hot_hbm, extra_hbm,
    send, pick_t, both, routes_in, combine_in, hot, extra, sems,
):
    count = tok_hbm.shape[0]
    copies = [
        pltpu.make_async_copy(source, target, sems.at[i])
        for i, (source, target) in enumerate(
            [
                (routes_hbm, routes_in),
                (combine_hbm, combine_in),
                (hot_hbm, hot),
                (extra_hbm, extra),
                (tok_hbm, both.at[pl.ds(0, count)]),
                (cot_hbm, both.at[pl.ds(count, count)]),
            ]
        )
    ]
    for copy in copies:
        copy.start()
    for copy in copies[:4]:
        copy.wait()
    lanes = 2 * count
    src = lax.broadcasted_iota(jnp.int32, (count, lanes), 0)
    dst = lax.broadcasted_iota(jnp.int32, (count, lanes), 1)
    dst = jnp.where(dst >= count, dst - count, dst)
    twice = jnp.where(src == dst, 1.0, 0.0).astype(BF16)
    routes = dot(routes_in[...].astype(F32).astype(BF16), twice, NN)
    combine = dot(combine_in[...], twice, NN)
    expert_id = lax.broadcasted_iota(jnp.int32, (experts, lanes), 0)
    lane = lax.broadcasted_iota(jnp.int32, (experts, lanes), 1)
    named = jnp.zeros((experts, lanes), F32)
    weight = jnp.zeros((experts, lanes), F32)
    expert_number = expert_id.astype(F32)
    for k in range(routes.shape[0]):
        match = expert_number == routes[k : k + 1, :]
        named = named + jnp.where(match, 1.0, 0.0)
        weight = weight + jnp.where(match, combine[k : k + 1, :], 0.0)
    before = jnp.where(src < dst, 1.0, 0.0).astype(BF16)
    rank = dot(named[:, :count].astype(BF16), before, NN)
    limit = jnp.full((experts, lanes), float(BASE), F32)
    for j in range(hot.shape[0]):
        limit = limit + jnp.where(expert_id == hot[j], extra[j].astype(F32), 0.0)
    place = jnp.where(lane >= count, rank + float(SLOTS), rank)
    place = jnp.where(named > 0.5, place, -1.0)
    place = jnp.where(rank < limit, place, -1.0)
    weight = jnp.where(lane >= count, weight, 1.0)
    slot = lax.broadcasted_iota(jnp.int32, (experts, MSG, lanes), 1).astype(F32)
    hit = jnp.broadcast_to(place[:, None, :], (experts, MSG, lanes)) == slot
    scaled = jnp.where(hit, jnp.broadcast_to(weight[:, None, :], hit.shape), 0.0)
    scaled = scaled.reshape(experts * MSG, lanes).astype(BF16)
    for copy in copies[4:]:
        copy.wait()
    send[...] = jnp.dot(scaled, both[...], preferred_element_type=F32).astype(BF16)
    pick = jnp.where(hit, 1.0, 0.0).reshape(experts * MSG, lanes).astype(BF16)
    pick_t[...] = dot(identity(lanes), pick, NT).astype(BF16)


def token_body(pick_t, returned, out):
    count, half = out.shape[0], returned.shape[1]
    both = dot(pick_t[...], returned[...], NN)
    out[:, :half] = both[:count].astype(BF16)
    out[:, half:] = both[count:].astype(BF16)


def pack(half_down, buffer):
    rows, width = half_down.shape
    wide = 3 * width // 4
    extra = rows // 3
    buffer[:rows, :wide] = half_down[:, :wide]
    for k in range(3):
        cols = slice(k * (width - wide), (k + 1) * (width - wide))
        buffer[rows:, cols] = half_down[k * extra : (k + 1) * extra, wide:]


def add(kept, received):
    return kept.astype(F32) + received.astype(F32)


def middle_body(send, keep, received, out):
    wide = keep.shape[1]
    narrow = wide // 2
    out[:, :wide] = add(send[:, :wide], received[:, :wide]).astype(BF16)
    out[:, wide:] = add(keep[:, :narrow], received[:, wide : wide + narrow]).astype(BF16)


def final_body(
    even_keep, even_first, even_sum, even_second, mirror_keep, mirror_first, mirror_sum, mirror_second,
    grad_gate, grad_up, grad_down,
):
    hidden, width = grad_down.shape
    cut, wide = hidden // 2, 3 * width // 4
    extra = cut // 3
    for top, keep, first, middle, second, out in (
        (0, even_keep, even_first, even_sum, even_second, grad_up),
        (cut, mirror_keep, mirror_first, mirror_sum, mirror_second, grad_gate),
    ):
        down = add(middle[:, :wide], second[:, :wide]).astype(BF16)
        grad_down[top : top + cut, :wide] = down[:cut]
        for k in range(3):
            cols = slice(k * (width - wide), (k + 1) * (width - wide))
            grad_down[top + k * extra : top + (k + 1) * extra, wide:] = down[cut:, cols]
        own = add(keep[:, hidden:], first[:, wide + hidden :])
        out[...] = add(own, second[:, wide:]).astype(BF16)


def expert_body(
    ranks, me, recv_hbm, w_gate_hbm, w_up_hbm, w_down_hbm,
    back_hbm, even_send_hbm, mirror_send_hbm, even_keep_hbm, mirror_keep_hbm,
    recv, w_in, w_down,
    back, even_send, mirror_send, even_keep, mirror_keep,
    wide, narrow, tok, og, pre, grad, in_rows, hid, total, in_sems, out_sems,
):
    rows_in, features = recv.shape
    hidden = w_down.shape[0]
    peers = rows_in // MSG
    half = features // 2
    step = rows_in // CHUNKS
    arrivals = []
    for n in range(CHUNKS):
        at = pl.ds(n * step, step)
        arrivals.append(pltpu.make_async_copy(recv_hbm.at[at], recv.at[at], in_sems.at[n]))
    for n, (source, target) in enumerate(
        [
            (w_gate_hbm, w_in.at[:, pl.ds(0, hidden)]),
            (w_up_hbm, w_in.at[:, pl.ds(hidden, hidden)]),
            (w_down_hbm, w_down),
        ]
    ):
        arrivals.append(pltpu.make_async_copy(source, target, in_sems.at[CHUNKS + n]))
    for copy in arrivals:
        copy.start()
    departures = []

    def send_out(source, target):
        copy = pltpu.make_async_copy(source, target, out_sems.at[len(departures)])
        copy.start()
        departures.append(copy)

    for n in range(CHUNKS):
        arrivals[n].wait()
        at = pl.ds(n * step, step)
        for c in range(features // LANES):
            wide[c, at, :] = recv[at, c * LANES : (c + 1) * LANES].astype(F32)
    for s in range(SLOTS):
        at = pl.ds(s * peers, peers)
        for c in range(features // LANES):
            cols = slice(c * LANES, (c + 1) * LANES)
            tok[at, cols] = wide[c, pl.ds(s, peers, MSG), :].astype(BF16)
            og[at, cols] = wide[c, pl.ds(s + SLOTS, peers, MSG), :].astype(BF16)
    for copy in arrivals[CHUNKS:]:
        copy.wait()
    for first in range(0, SLOTS * peers, 512):
        span = slice(first, first + 512)
        pre[span, :] = dot(tok[span, :], w_in[...], NN)
        grad[span, :] = dot(og[span, :], w_down[...], NT)
        for at in range(first, first + 512, 128):
            rows = slice(at, at + 128)
            gate_pre, up_proj, hidden_grad = pre[rows, :hidden], pre[rows, hidden:], grad[rows, :]
            s = jax.nn.sigmoid(gate_pre)
            act = gate_pre * s
            hid[rows, :] = (act * up_proj).astype(BF16)
            gate_grad = hidden_grad * up_proj * s * (1.0 + gate_pre * (1.0 - s))
            in_rows[rows, :hidden] = gate_grad.astype(BF16)
            in_rows[rows, hidden:] = (hidden_grad * act).astype(BF16)
        grads = dot(in_rows[span, :], w_in[...], NT)
        for s in range(first // peers, (first + 512) // peers):
            piece = grads[s * peers - first : (s + 1) * peers - first, :]
            for c in range(half // LANES):
                low = piece[:, c * LANES : (c + 1) * LANES]
                high = piece[:, half + c * LANES : half + (c + 1) * LANES]
                narrow[c, pl.ds(s, peers, MSG), :] = low
                narrow[c, pl.ds(s + SLOTS, peers, MSG), :] = high
    for c in range(half // LANES):
        back[:, c * LANES : (c + 1) * LANES] = narrow[c].astype(BF16)
    send_out(back, back_hbm)
    down = dot(hid[...], og[...], TN).astype(BF16)
    cut = hidden // 2
    pack(down[:cut], even_send)
    pack(down[cut:], mirror_send)
    total[...] = dot(tok[...], in_rows[...], TN)
    piece = features // ranks
    even = me[0] + 1 - 2 * lax.rem(me[0], 2)
    mirror = ranks - 1 - me[0]
    opposite = ranks - 1 - even
    for cols, keep, send, keep_hbm, send_hbm, here, other in (
        (slice(hidden, 2 * hidden), even_keep, even_send, even_keep_hbm, even_send_hbm, even, mirror),
        (slice(0, hidden), mirror_keep, mirror_send, mirror_keep_hbm, mirror_send_hbm, mirror, even),
    ):

        def part_of(index):
            return total[pl.ds(pl.multiple_of(index * piece, 16), piece), cols].astype(BF16)

        send[:, 2 * hidden : 3 * hidden] = part_of(opposite)
        send[:, 3 * hidden :] = part_of(here)
        send_out(send, send_hbm)
        keep[:, :hidden] = part_of(other)
        keep[:, hidden:] = part_of(me[0])
        send_out(keep, keep_hbm)
    for copy in departures:
        copy.wait()


def shards(tokens, cotangent, routes, combine, hot_experts, extra_slots, w_gate, w_up, w_down):
    experts = lax.axis_size("expert")
    ranks = lax.axis_size("dp")
    count, features = tokens.shape
    hidden = w_gate.shape[2]
    total = experts * MSG
    rows = experts * SLOTS
    send, pick_t = call(
        functools.partial(dispatch_body, experts),
        "dispatch",
        [
            jax.ShapeDtypeStruct((total, features), BF16),
            jax.ShapeDtypeStruct((2 * count, total), BF16),
        ],
        [ANY] * 6,
        [
            pltpu.VMEM((2 * count, features), BF16),
            pltpu.VMEM(routes.shape[::-1], jnp.int32),
            pltpu.VMEM(combine.shape[::-1], BF16),
            pltpu.SMEM(hot_experts.shape, jnp.int32),
            pltpu.SMEM(extra_slots.shape, jnp.int32),
            pltpu.SemaphoreType.DMA((6,)),
        ],
        2 * total * 2 * count * features,
        2 * total * features,
        64 * MIB - 65536,
    )(tokens, cotangent, routes.T, combine.T, hot_experts, extra_slots)
    recv = lax.all_to_all(send, "expert", split_axis=0, concat_axis=0, tiled=True)
    me = lax.axis_index("dp").astype(jnp.int32).reshape(1)
    piece = features // ranks
    packed = jax.ShapeDtypeStruct((piece, 4 * hidden), BF16)
    kept = jax.ShapeDtypeStruct((piece, 2 * hidden), BF16)
    pieces = [jax.ShapeDtypeStruct((total, features // 2), BF16), packed, packed, kept, kept]
    back, even_send, mirror_send, even_keep, mirror_keep = call(
        functools.partial(expert_body, ranks),
        "expert",
        pieces,
        [SMEM] + [ANY] * 4,
        [
            pltpu.VMEM((total, features), BF16),
            pltpu.VMEM((features, 2 * hidden), BF16),
            pltpu.VMEM((hidden, features), BF16),
        ]
        + [pltpu.VMEM(a.shape, a.dtype) for a in pieces]
        + [
            pltpu.VMEM((features // LANES, total, LANES), F32),
            pltpu.VMEM((features // 2 // LANES, total, LANES), F32),
            pltpu.VMEM((rows, features), BF16),
            pltpu.VMEM((rows, features), BF16),
            pltpu.VMEM((rows, 2 * hidden), F32),
            pltpu.VMEM((rows, hidden), F32),
            pltpu.VMEM((rows, 2 * hidden), BF16),
            pltpu.VMEM((rows, hidden), BF16),
            pltpu.VMEM((features, 2 * hidden), F32),
            pltpu.SemaphoreType.DMA((CHUNKS + 3,)),
            pltpu.SemaphoreType.DMA((len(pieces),)),
        ],
        16 * rows * features * hidden,
        2 * (total * features * 2 + 6 * features * hidden),
        64 * MIB - 65536,
        ANY,
    )(me, recv, w_gate[0], w_up[0], w_down[0])
    returned = lax.all_to_all(back, "expert", split_axis=0, concat_axis=0, tiled=True)

    def even(value):
        return lax.ppermute(value, "dp", [(i, i ^ 1) for i in range(ranks)])

    def mirror(value):
        return lax.ppermute(value, "dp", [(i, ranks - 1 - i) for i in range(ranks)])

    def middle(send, keep, received):
        return call(
            middle_body,
            "middle",
            jax.ShapeDtypeStruct((piece, 3 * hidden), BF16),
            [VMEM] * 3,
            (),
            2 * piece * 3 * hidden,
            6 * piece * 4 * hidden,
        )(send, keep, received)

    even_first, mirror_first = even(even_send), mirror(mirror_send)
    even_sum = middle(even_send, even_keep, even_first)
    even_second = mirror(even_sum)
    mirror_sum = middle(mirror_send, mirror_keep, mirror_first)
    mirror_second = even(mirror_sum)
    grad_gate, grad_up, grad_down = call(
        final_body,
        "final",
        [
            jax.ShapeDtypeStruct((piece, hidden), BF16),
            jax.ShapeDtypeStruct((piece, hidden), BF16),
            jax.ShapeDtypeStruct((hidden, features), BF16),
        ],
        [VMEM] * 8,
        (),
        4 * piece * 4 * hidden,
        12 * piece * 4 * hidden,
    )(
        even_keep, even_first, even_sum, even_second,
        mirror_keep, mirror_first, mirror_sum, mirror_second,
    )
    token_grads = call(
        token_body,
        "token_grad",
        jax.ShapeDtypeStruct((count, features), BF16),
        [VMEM, VMEM],
        (),
        2 * total * count * features,
        2 * total * features,
    )(pick_t, returned)
    return token_grads, grad_gate[None], grad_up[None], grad_down[None]


def solution(mesh):
    in_specs = (
        P(("dp", "expert"), None),
        P(("dp", "expert"), None),
        P(("dp", "expert"), None),
        P(("dp", "expert"), None),
        P(),
        P(),
        P("expert", None, None),
        P("expert", None, None),
        P("expert", None, None),
    )
    out_specs = (
        P(("dp", "expert"), None),
        P("expert", "dp", None),
        P("expert", "dp", None),
        P("expert", None, None),
    )
    return jax.shard_map(shards, mesh=mesh, in_specs=in_specs, out_specs=out_specs, check_vma=False)
```

```python
import functools

import jax
import jax.numpy as jnp
from jax import lax
from jax.experimental import pallas as pl
from jax.experimental.pallas import tpu as pltpu
from jax.sharding import PartitionSpec as P

BASE = 2
SLOTS = 4
MSG = 2 * SLOTS
LANES = 128
CHUNKS = 4
F32 = jnp.float32
BF16 = jnp.bfloat16
VMEM = pl.BlockSpec(memory_space=pltpu.VMEM)
ANY = pl.BlockSpec(memory_space=pl.ANY)
SMEM = pl.BlockSpec(memory_space=pltpu.SMEM)
MIB = 1024 * 1024


NN = (((1,), (0,)), ((), ()))
NT = (((1,), (1,)), ((), ()))
TN = (((0,), (0,)), ((), ()))


def dot(a, b, dims):
    return lax.dot_general(a, b, dims, preferred_element_type=F32)


def call(
    body, name, out_shape, in_specs, scratch=(), flops=0, bytes_accessed=0, vmem=16 * MIB, out=VMEM
):
    return pl.pallas_call(
        body,
        name=name,
        out_shape=out_shape,
        in_specs=in_specs,
        out_specs=jax.tree.map(lambda _: out, out_shape),
        scratch_shapes=list(scratch),
        compiler_params=pltpu.CompilerParams(vmem_limit_bytes=vmem),
        cost_estimate=pl.CostEstimate(
            flops=flops, bytes_accessed=bytes_accessed, transcendentals=0
        ),
    )


def identity(n):
    rows = lax.broadcasted_iota(jnp.int32, (n, n), 0)
    return jnp.where(rows == lax.broadcasted_iota(jnp.int32, (n, n), 1), 1.0, 0.0).astype(BF16)


def dispatch_body(
    experts, tok_hbm, cot_hbm, routes_hbm, combine_hbm, hot_hbm, extra_hbm,
    send, pick_t, both, routes_in, combine_in, hot, extra, sems,
):
    count = tok_hbm.shape[0]
    copies = [
        pltpu.make_async_copy(source, target, sems.at[i])
        for i, (source, target) in enumerate(
            [
                (routes_hbm, routes_in),
                (combine_hbm, combine_in),
                (hot_hbm, hot),
                (extra_hbm, extra),
                (tok_hbm, both.at[pl.ds(0, count)]),
                (cot_hbm, both.at[pl.ds(count, count)]),
            ]
        )
    ]
    for copy in copies:
        copy.start()
    for copy in copies[:4]:
        copy.wait()
    lanes = 2 * count
    src = lax.broadcasted_iota(jnp.int32, (count, lanes), 0)
    dst = lax.broadcasted_iota(jnp.int32, (count, lanes), 1)
    dst = jnp.where(dst >= count, dst - count, dst)
    twice = jnp.where(src == dst, 1.0, 0.0).astype(BF16)
    routes = dot(routes_in[...].astype(F32).astype(BF16), twice, NN)
    combine = dot(combine_in[...], twice, NN)
    expert_id = lax.broadcasted_iota(jnp.int32, (experts, lanes), 0)
    lane = lax.broadcasted_iota(jnp.int32, (experts, lanes), 1)
    named = jnp.zeros((experts, lanes), F32)
    weight = jnp.zeros((experts, lanes), F32)
    expert_number = expert_id.astype(F32)
    for k in range(routes.shape[0]):
        match = expert_number == routes[k : k + 1, :]
        named = named + jnp.where(match, 1.0, 0.0)
        weight = weight + jnp.where(match, combine[k : k + 1, :], 0.0)
    before = jnp.where(src < dst, 1.0, 0.0).astype(BF16)
    rank = dot(named[:, :count].astype(BF16), before, NN)
    limit = jnp.full((experts, lanes), float(BASE), F32)
    for j in range(hot.shape[0]):
        limit = limit + jnp.where(expert_id == hot[j], extra[j].astype(F32), 0.0)
    place = jnp.where(lane >= count, rank + float(SLOTS), rank)
    place = jnp.where(named > 0.5, place, -1.0)
    place = jnp.where(rank < limit, place, -1.0)
    weight = jnp.where(lane >= count, weight, 1.0)
    slot = lax.broadcasted_iota(jnp.int32, (experts, MSG, lanes), 1).astype(F32)
    hit = jnp.broadcast_to(place[:, None, :], (experts, MSG, lanes)) == slot
    scaled = jnp.where(hit, jnp.broadcast_to(weight[:, None, :], hit.shape), 0.0)
    scaled = scaled.reshape(experts * MSG, lanes).astype(BF16)
    for copy in copies[4:]:
        copy.wait()
    send[...] = jnp.dot(scaled, both[...], preferred_element_type=F32).astype(BF16)
    pick = jnp.where(hit, 1.0, 0.0).reshape(experts * MSG, lanes).astype(BF16)
    pick_t[...] = dot(identity(lanes), pick, NT).astype(BF16)


def token_body(pick_t, returned, out):
    count, half = out.shape[0], returned.shape[1]
    both = dot(pick_t[...], returned[...], NN)
    out[:, :half] = both[:count].astype(BF16)
    out[:, half:] = both[count:].astype(BF16)


def start_all(copies):
    for copy in copies:
        copy.start()
    return copies


def wait_all(copies):
    for copy in copies:
        copy.wait()


def rows_body(
    recv_hbm, w_gate_hbm, w_up_hbm, w_down_hbm, back_hbm, tok_hbm, og_hbm, in_rows_hbm, hid_hbm,
    recv, w_in, w_down, back, tok, og, in_rows, hid, wide, narrow, pre, grad, in_sems, out_sems,
):
    rows_in, features = recv.shape
    hidden = w_down.shape[0]
    peers = rows_in // MSG
    half = features // 2
    step = rows_in // CHUNKS
    chunks = [pl.ds(n * step, step) for n in range(CHUNKS)]
    arrivals = start_all(
        [
            pltpu.make_async_copy(recv_hbm.at[at], recv.at[at], in_sems.at[n])
            for n, at in enumerate(chunks)
        ]
    )
    weights = start_all(
        [
            pltpu.make_async_copy(source, target, in_sems.at[CHUNKS + n])
            for n, (source, target) in enumerate(
                [
                    (w_gate_hbm, w_in.at[:, pl.ds(0, hidden)]),
                    (w_up_hbm, w_in.at[:, pl.ds(hidden, hidden)]),
                    (w_down_hbm, w_down),
                ]
            )
        ]
    )
    departures = []

    def send_out(source, target):
        copy = pltpu.make_async_copy(source, target, out_sems.at[len(departures)])
        departures.extend(start_all([copy]))

    for copy, at in zip(arrivals, chunks):
        copy.wait()
        for c in range(features // LANES):
            wide[c, at, :] = recv[at, c * LANES : (c + 1) * LANES].astype(F32)
    for s in range(SLOTS):
        at = pl.ds(s * peers, peers)
        for c in range(features // LANES):
            cols = slice(c * LANES, (c + 1) * LANES)
            tok[at, cols] = wide[c, pl.ds(s, peers, MSG), :].astype(BF16)
            og[at, cols] = wide[c, pl.ds(s + SLOTS, peers, MSG), :].astype(BF16)
    wait_all(weights)
    send_out(tok, tok_hbm)
    send_out(og, og_hbm)
    pre[...] = dot(tok[...], w_in[...], NN)
    grad[...] = dot(og[...], w_down[...], NT)
    for at in range(0, SLOTS * peers, peers):
        rows = slice(at, at + peers)
        gate_pre, up_proj, hidden_grad = pre[rows, :hidden], pre[rows, hidden:], grad[rows, :]
        s = jax.nn.sigmoid(gate_pre)
        act = gate_pre * s
        hid[rows, :] = (act * up_proj).astype(BF16)
        gate_grad = hidden_grad * up_proj * s * (1.0 + gate_pre * (1.0 - s))
        in_rows[rows, :hidden] = gate_grad.astype(BF16)
        in_rows[rows, hidden:] = (hidden_grad * act).astype(BF16)
    send_out(hid, hid_hbm)
    send_out(in_rows, in_rows_hbm)
    grads = dot(in_rows[...], w_in[...], NT)
    for s in range(SLOTS):
        piece = grads[s * peers : (s + 1) * peers, :]
        for c in range(half // LANES):
            low = piece[:, c * LANES : (c + 1) * LANES]
            high = piece[:, half + c * LANES : half + (c + 1) * LANES]
            narrow[c, pl.ds(s, peers, MSG), :] = low
            narrow[c, pl.ds(s + SLOTS, peers, MSG), :] = high
    for c in range(half // LANES):
        back[:, c * LANES : (c + 1) * LANES] = narrow[c].astype(BF16)
    send_out(back, back_hbm)
    wait_all(departures)


def weights_body(
    ranks, me, tok_hbm, og_hbm, in_rows_hbm, hid_hbm,
    down_a_hbm, down_b_hbm, even_send_hbm, mirror_send_hbm, even_keep_hbm, mirror_keep_hbm,
    tok, og, in_rows, hid,
    down_a, down_b, even_send, mirror_send, even_keep, mirror_keep,
    total, in_sems, out_sems,
):
    features, hidden = tok.shape[1], hid.shape[1]
    arrivals = start_all(
        [
            pltpu.make_async_copy(source, target, in_sems.at[n])
            for n, (source, target) in enumerate(
                [(hid_hbm, hid), (og_hbm, og), (tok_hbm, tok), (in_rows_hbm, in_rows)]
            )
        ]
    )
    departures = []

    def send_out(source, target):
        copy = pltpu.make_async_copy(source, target, out_sems.at[len(departures)])
        departures.extend(start_all([copy]))

    wait_all(arrivals[:2])
    down = dot(hid[...], og[...], TN).astype(BF16)
    cut = hidden // 2
    down_a[...] = down[:cut]
    send_out(down_a, down_a_hbm)
    down_b[...] = down[cut:]
    send_out(down_b, down_b_hbm)
    wait_all(arrivals[2:])
    total[...] = dot(tok[...], in_rows[...], TN)
    piece = features // ranks
    even = me[0] + 1 - 2 * lax.rem(me[0], 2)
    mirror = ranks - 1 - me[0]
    opposite = ranks - 1 - even
    for cols, keep, send, keep_hbm, send_hbm, here, other in (
        (slice(hidden, 2 * hidden), even_keep, even_send, even_keep_hbm, even_send_hbm, even, mirror),
        (slice(0, hidden), mirror_keep, mirror_send, mirror_keep_hbm, mirror_send_hbm, mirror, even),
    ):

        def part_of(index):
            return total[pl.ds(pl.multiple_of(index * piece, 16), piece), cols].astype(BF16)

        send[:, :hidden] = part_of(opposite)
        send[:, hidden:] = part_of(here)
        send_out(send, send_hbm)
        keep[:, :hidden] = part_of(other)
        keep[:, hidden:] = part_of(me[0])
        send_out(keep, keep_hbm)
    wait_all(departures)


def add(kept, received):
    return kept.astype(F32) + received.astype(F32)


def sum_body(kept, received, out):
    width = out.shape[1]
    out[...] = add(kept[:, :width], received[:, :width]).astype(BF16)


def down_body(sum_a, next_a, sum_b, next_b, out):
    cut = sum_a.shape[0]
    out[:cut, :] = add(sum_a[...], next_a[...]).astype(BF16)
    out[cut:, :] = add(sum_b[...], next_b[...]).astype(BF16)


def pair_body(gate_keep, gate_first, gate_next, up_keep, up_first, up_next, grad_gate, grad_up):
    hidden = grad_gate.shape[1]
    gate = add(gate_keep[:, hidden:], gate_first[:, hidden:]) + gate_next[...].astype(F32)
    up = add(up_keep[:, hidden:], up_first[:, hidden:]) + up_next[...].astype(F32)
    grad_gate[...] = gate.astype(BF16)
    grad_up[...] = up.astype(BF16)


def shards(tokens, cotangent, routes, combine, hot_experts, extra_slots, w_gate, w_up, w_down):
    experts = lax.axis_size("expert")
    ranks = lax.axis_size("dp")
    count, features = tokens.shape
    hidden = w_gate.shape[2]
    total = experts * MSG
    rows = experts * SLOTS
    send, pick_t = call(
        functools.partial(dispatch_body, experts),
        "dispatch",
        [
            jax.ShapeDtypeStruct((total, features), BF16),
            jax.ShapeDtypeStruct((2 * count, total), BF16),
        ],
        [ANY] * 6,
        [
            pltpu.VMEM((2 * count, features), BF16),
            pltpu.VMEM(routes.shape[::-1], jnp.int32),
            pltpu.VMEM(combine.shape[::-1], BF16),
            pltpu.SMEM(hot_experts.shape, jnp.int32),
            pltpu.SMEM(extra_slots.shape, jnp.int32),
            pltpu.SemaphoreType.DMA((6,)),
        ],
        2 * total * 2 * count * features,
        2 * total * features,
        64 * MIB - 65536,
    )(tokens, cotangent, routes.T, combine.T, hot_experts, extra_slots)
    recv = lax.all_to_all(send, "expert", split_axis=0, concat_axis=0, tiled=True)
    me = lax.axis_index("dp").astype(jnp.int32).reshape(1)
    piece = features // ranks
    cut = hidden // 2
    shape = jax.ShapeDtypeStruct
    saved = [
        shape((rows, features), BF16),
        shape((rows, features), BF16),
        shape((rows, 2 * hidden), BF16),
        shape((rows, hidden), BF16),
    ]
    out = [shape((total, features // 2), BF16)] + saved
    back, *kept_rows = call(
        rows_body,
        "rows",
        out,
        [ANY] * 4,
        [
            pltpu.VMEM((total, features), BF16),
            pltpu.VMEM((features, 2 * hidden), BF16),
            pltpu.VMEM((hidden, features), BF16),
        ]
        + [pltpu.VMEM(a.shape, a.dtype) for a in out]
        + [
            pltpu.VMEM((features // LANES, total, LANES), F32),
            pltpu.VMEM((features // 2 // LANES, total, LANES), F32),
            pltpu.VMEM((rows, 2 * hidden), F32),
            pltpu.VMEM((rows, hidden), F32),
            pltpu.SemaphoreType.DMA((CHUNKS + 3,)),
            pltpu.SemaphoreType.DMA((len(out),)),
        ],
        10 * rows * features * hidden,
        2 * (total * features * 2 + 3 * features * hidden),
        64 * MIB - 65536,
        ANY,
    )(recv, w_gate[0], w_up[0], w_down[0])
    returned = lax.all_to_all(back, "expert", split_axis=0, concat_axis=0, tiled=True)
    out = [shape((cut, features), BF16)] * 2 + [shape((piece, 2 * hidden), BF16)] * 4
    down_a, down_b, even_send, mirror_send, even_keep, mirror_keep = call(
        functools.partial(weights_body, ranks),
        "weight_grads",
        out,
        [SMEM] + [ANY] * 4,
        [pltpu.VMEM(a.shape, a.dtype) for a in saved]
        + [pltpu.VMEM(a.shape, a.dtype) for a in out]
        + [
            pltpu.VMEM((features, 2 * hidden), F32),
            pltpu.SemaphoreType.DMA((len(saved),)),
            pltpu.SemaphoreType.DMA((len(out),)),
        ],
        6 * rows * features * hidden,
        2 * (rows * (2 * features + 3 * hidden) + 3 * features * hidden),
        64 * MIB - 65536,
        ANY,
    )(me, *kept_rows)

    def even(value):
        return lax.ppermute(value, "dp", [(i, i ^ 1) for i in range(ranks)])

    def mirror(value):
        return lax.ppermute(value, "dp", [(i, ranks - 1 - i) for i in range(ranks)])

    def small(body, name, out, *operands):
        return call(body, name, out, [VMEM] * len(operands))(*operands)

    first_a, first_b = even(down_a), mirror(down_b)
    up_first, gate_first = even(even_send), mirror(mirror_send)
    half_down = shape((cut, features), BF16)
    one_piece = shape((piece, hidden), BF16)
    sum_a = small(sum_body, "down_a", half_down, down_a, first_a)
    next_a = mirror(sum_a)
    sum_b = small(sum_body, "down_b", half_down, down_b, first_b)
    next_b = even(sum_b)
    up_next = mirror(small(sum_body, "up", one_piece, even_keep, up_first))
    gate_next = even(small(sum_body, "gate", one_piece, mirror_keep, gate_first))
    grad_down = small(
        down_body, "down", shape((hidden, features), BF16), sum_a, next_a, sum_b, next_b
    )
    grad_gate, grad_up = small(
        pair_body,
        "pair",
        [one_piece, one_piece],
        mirror_keep, gate_first, gate_next, even_keep, up_first, up_next,
    )
    token_grads = call(
        token_body,
        "token_grad",
        jax.ShapeDtypeStruct((count, features), BF16),
        [VMEM, VMEM],
        (),
        2 * total * count * features,
        2 * total * features,
    )(pick_t, returned)
    return token_grads, grad_gate[None], grad_up[None], grad_down[None]


def solution(mesh):
    in_specs = (
        P(("dp", "expert"), None),
        P(("dp", "expert"), None),
        P(("dp", "expert"), None),
        P(("dp", "expert"), None),
        P(),
        P(),
        P("expert", None, None),
        P("expert", None, None),
        P("expert", None, None),
    )
    out_specs = (
        P(("dp", "expert"), None),
        P("expert", "dp", None),
        P("expert", "dp", None),
        P("expert", None, None),
    )
    return jax.shard_map(shards, mesh=mesh, in_specs=in_specs, out_specs=out_specs, check_vma=False)
```

```python
import functools

import jax
import jax.numpy as jnp
from jax import lax
from jax.experimental import pallas as pl
from jax.experimental.pallas import tpu as pltpu
from jax.sharding import PartitionSpec as P

BASE = 2
SLOTS = 4
MSG = 2 * SLOTS
LANES = 128
CHUNKS = 4
F32 = jnp.float32
BF16 = jnp.bfloat16
VMEM = pl.BlockSpec(memory_space=pltpu.VMEM)
ANY = pl.BlockSpec(memory_space=pl.ANY)
SMEM = pl.BlockSpec(memory_space=pltpu.SMEM)
MIB = 1024 * 1024


NN = (((1,), (0,)), ((), ()))
NT = (((1,), (1,)), ((), ()))
TN = (((0,), (0,)), ((), ()))


def dot(a, b, dims):
    return lax.dot_general(a, b, dims, preferred_element_type=F32)


def call(
    body, name, out_shape, in_specs, scratch=(), flops=0, bytes_accessed=0, vmem=16 * MIB, out=VMEM
):
    return pl.pallas_call(
        body,
        name=name,
        out_shape=out_shape,
        in_specs=in_specs,
        out_specs=jax.tree.map(lambda _: out, out_shape),
        scratch_shapes=list(scratch),
        compiler_params=pltpu.CompilerParams(vmem_limit_bytes=vmem),
        cost_estimate=pl.CostEstimate(
            flops=flops, bytes_accessed=bytes_accessed, transcendentals=0
        ),
    )


def identity(n):
    rows = lax.broadcasted_iota(jnp.int32, (n, n), 0)
    return jnp.where(rows == lax.broadcasted_iota(jnp.int32, (n, n), 1), 1.0, 0.0).astype(BF16)


def dispatch_body(
    experts, tok_hbm, cot_hbm, routes_hbm, combine_hbm, hot_hbm, extra_hbm,
    send_hbm, pick_hbm, send, pick_t, both, routes_in, combine_in, hot, extra, sems, out_sems,
):
    count = tok_hbm.shape[0]
    copies = [
        pltpu.make_async_copy(source, target, sems.at[i])
        for i, (source, target) in enumerate(
            [
                (routes_hbm, routes_in),
                (combine_hbm, combine_in),
                (hot_hbm, hot),
                (extra_hbm, extra),
                (tok_hbm, both.at[pl.ds(0, count)]),
                (cot_hbm, both.at[pl.ds(count, count)]),
            ]
        )
    ]
    for copy in copies:
        copy.start()
    for copy in copies[:4]:
        copy.wait()
    lanes = 2 * count
    src = lax.broadcasted_iota(jnp.int32, (count, lanes), 0)
    dst = lax.broadcasted_iota(jnp.int32, (count, lanes), 1)
    dst = jnp.where(dst >= count, dst - count, dst)
    twice = jnp.where(src == dst, 1.0, 0.0).astype(BF16)
    routes = dot(routes_in[...].astype(F32).astype(BF16), twice, NN)
    combine = dot(combine_in[...], twice, NN)
    expert_id = lax.broadcasted_iota(jnp.int32, (experts, lanes), 0)
    lane = lax.broadcasted_iota(jnp.int32, (experts, lanes), 1)
    named = jnp.zeros((experts, lanes), F32)
    weight = jnp.zeros((experts, lanes), F32)
    expert_number = expert_id.astype(F32)
    for k in range(routes.shape[0]):
        match = expert_number == routes[k : k + 1, :]
        named = named + jnp.where(match, 1.0, 0.0)
        weight = weight + jnp.where(match, combine[k : k + 1, :], 0.0)
    before = jnp.where(src < dst, 1.0, 0.0).astype(BF16)
    rank = dot(named[:, :count].astype(BF16), before, NN)
    limit = jnp.full((experts, lanes), float(BASE), F32)
    for j in range(hot.shape[0]):
        limit = limit + jnp.where(expert_id == hot[j], extra[j].astype(F32), 0.0)
    place = jnp.where(lane >= count, rank + float(SLOTS), rank)
    place = jnp.where(named > 0.5, place, -1.0)
    place = jnp.where(rank < limit, place, -1.0)
    weight = jnp.where(lane >= count, weight, 1.0)
    slot = lax.broadcasted_iota(jnp.int32, (experts, MSG, lanes), 1).astype(F32)
    hit = jnp.broadcast_to(place[:, None, :], (experts, MSG, lanes)) == slot
    scaled = jnp.where(hit, jnp.broadcast_to(weight[:, None, :], hit.shape), 0.0)
    scaled = scaled.reshape(experts * MSG, lanes).astype(BF16)
    for copy in copies[4:]:
        copy.wait()
    part = send.shape[0] // CHUNKS
    departures = []
    for n in range(CHUNKS):
        at = pl.ds(n * part, part)
        block = dot(scaled[n * part : (n + 1) * part, :], both[...], NN)
        send[at, :] = block.astype(BF16)
        departures += start_all([pltpu.make_async_copy(send.at[at], send_hbm.at[at], out_sems.at[n])])
    pick = jnp.where(hit, 1.0, 0.0).reshape(experts * MSG, lanes).astype(BF16)
    pick_t[...] = dot(identity(lanes), pick, NT).astype(BF16)
    departures += start_all([pltpu.make_async_copy(pick_t, pick_hbm, out_sems.at[CHUNKS])])
    wait_all(departures)


def token_body(pick_t, returned, out):
    count, half = out.shape[0], returned.shape[1]
    both = dot(pick_t[...], returned[...], NN)
    out[:, :half] = both[:count].astype(BF16)
    out[:, half:] = both[count:].astype(BF16)


def start_all(copies):
    for copy in copies:
        copy.start()
    return copies


def wait_all(copies):
    for copy in copies:
        copy.wait()


def expert_body(
    ranks, me, recv_hbm, w_gate_hbm, w_up_hbm, w_down_hbm,
    back_hbm, down_a_hbm, down_b_hbm, even_send_hbm, mirror_send_hbm, even_keep_hbm, mirror_keep_hbm,
    back, down_a, down_b, even_send, mirror_send, even_keep, mirror_keep,
    recv, w_in, w_down, wide, narrow, tok, og, pre, grad, in_rows, hid, total, in_sems, out_sems,
):
    rows_in, features = recv.shape
    hidden = w_down.shape[0]
    peers = rows_in // MSG
    half = features // 2
    step = rows_in // CHUNKS
    chunks = [pl.ds(n * step, step) for n in range(CHUNKS)]
    arrivals = start_all(
        [
            pltpu.make_async_copy(recv_hbm.at[at], recv.at[at], in_sems.at[n])
            for n, at in enumerate(chunks)
        ]
    )
    weights = start_all(
        [
            pltpu.make_async_copy(source, target, in_sems.at[CHUNKS + n])
            for n, (source, target) in enumerate(
                [
                    (w_gate_hbm, w_in.at[:, pl.ds(0, hidden)]),
                    (w_up_hbm, w_in.at[:, pl.ds(hidden, hidden)]),
                    (w_down_hbm, w_down),
                ]
            )
        ]
    )
    departures = []

    def send_out(source, target):
        copy = pltpu.make_async_copy(source, target, out_sems.at[len(departures)])
        departures.extend(start_all([copy]))

    for copy, at in zip(arrivals, chunks):
        copy.wait()
        for c in range(features // LANES):
            wide[c, at, :] = recv[at, c * LANES : (c + 1) * LANES].astype(F32)
    for s in range(SLOTS):
        at = pl.ds(s * peers, peers)
        for c in range(features // LANES):
            cols = slice(c * LANES, (c + 1) * LANES)
            tok[at, cols] = wide[c, pl.ds(s, peers, MSG), :].astype(BF16)
            og[at, cols] = wide[c, pl.ds(s + SLOTS, peers, MSG), :].astype(BF16)
    wait_all(weights)
    pre[...] = dot(tok[...], w_in[...], NN)
    grad[...] = dot(og[...], w_down[...], NT)
    for at in range(0, SLOTS * peers, peers):
        rows = slice(at, at + peers)
        gate_pre, up_proj, hidden_grad = pre[rows, :hidden], pre[rows, hidden:], grad[rows, :]
        s = jax.nn.sigmoid(gate_pre)
        act = gate_pre * s
        hid[rows, :] = (act * up_proj).astype(BF16)
        gate_grad = hidden_grad * up_proj * s * (1.0 + gate_pre * (1.0 - s))
        in_rows[rows, :hidden] = gate_grad.astype(BF16)
        in_rows[rows, hidden:] = (hidden_grad * act).astype(BF16)
    grads = dot(in_rows[...], w_in[...], NT)
    for s in range(SLOTS):
        piece = grads[s * peers : (s + 1) * peers, :]
        for c in range(half // LANES):
            low = piece[:, c * LANES : (c + 1) * LANES]
            high = piece[:, half + c * LANES : half + (c + 1) * LANES]
            narrow[c, pl.ds(s, peers, MSG), :] = low
            narrow[c, pl.ds(s + SLOTS, peers, MSG), :] = high
    for c in range(half // LANES):
        back[:, c * LANES : (c + 1) * LANES] = narrow[c].astype(BF16)
    send_out(back, back_hbm)
    total[...] = dot(tok[...], in_rows[...], TN)
    piece = features // ranks
    even = me[0] + 1 - 2 * lax.rem(me[0], 2)
    mirror = ranks - 1 - me[0]
    opposite = ranks - 1 - even
    for cols, keep, send, keep_hbm, send_hbm, here, other in (
        (slice(hidden, 2 * hidden), even_keep, even_send, even_keep_hbm, even_send_hbm, even, mirror),
        (slice(0, hidden), mirror_keep, mirror_send, mirror_keep_hbm, mirror_send_hbm, mirror, even),
    ):

        def part_of(index):
            return total[pl.ds(pl.multiple_of(index * piece, 16), piece), cols].astype(BF16)

        send[:, :hidden] = part_of(opposite)
        send[:, hidden:] = part_of(here)
        send_out(send, send_hbm)
        keep[:, :hidden] = part_of(other)
        keep[:, hidden:] = part_of(me[0])
        send_out(keep, keep_hbm)
    down = dot(hid[...], og[...], TN).astype(BF16)
    cut = hidden // 2
    down_a[...] = down[:cut]
    send_out(down_a, down_a_hbm)
    down_b[...] = down[cut:]
    send_out(down_b, down_b_hbm)
    wait_all(departures)


def add(kept, received):
    return kept.astype(F32) + received.astype(F32)


def sum_body(kept, received, out):
    width = out.shape[1]
    out[...] = add(kept[:, :width], received[:, :width]).astype(BF16)


def down_body(sum_a, next_a, sum_b, next_b, out):
    cut = sum_a.shape[0]
    out[:cut, :] = add(sum_a[...], next_a[...]).astype(BF16)
    out[cut:, :] = add(sum_b[...], next_b[...]).astype(BF16)


def pair_body(gate_keep, gate_first, gate_next, up_keep, up_first, up_next, grad_gate, grad_up):
    hidden = grad_gate.shape[1]
    gate = add(gate_keep[:, hidden:], gate_first[:, hidden:]) + gate_next[...].astype(F32)
    up = add(up_keep[:, hidden:], up_first[:, hidden:]) + up_next[...].astype(F32)
    grad_gate[...] = gate.astype(BF16)
    grad_up[...] = up.astype(BF16)


def shards(tokens, cotangent, routes, combine, hot_experts, extra_slots, w_gate, w_up, w_down):
    experts = lax.axis_size("expert")
    ranks = lax.axis_size("dp")
    count, features = tokens.shape
    hidden = w_gate.shape[2]
    total = experts * MSG
    rows = experts * SLOTS
    me = lax.axis_index("dp").astype(jnp.int32).reshape(1)
    me, hot_experts = lax.optimization_barrier((me, hot_experts))
    send, pick_t = call(
        functools.partial(dispatch_body, experts),
        "dispatch",
        [
            jax.ShapeDtypeStruct((total, features), BF16),
            jax.ShapeDtypeStruct((2 * count, total), BF16),
        ],
        [ANY] * 6,
        [
            pltpu.VMEM((total, features), BF16),
            pltpu.VMEM((2 * count, total), BF16),
            pltpu.VMEM((2 * count, features), BF16),
            pltpu.VMEM(routes.shape[::-1], jnp.int32),
            pltpu.VMEM(combine.shape[::-1], BF16),
            pltpu.SMEM(hot_experts.shape, jnp.int32),
            pltpu.SMEM(extra_slots.shape, jnp.int32),
            pltpu.SemaphoreType.DMA((6,)),
            pltpu.SemaphoreType.DMA((CHUNKS + 1,)),
        ],
        2 * total * 2 * count * features,
        2 * total * features,
        64 * MIB - 65536,
        ANY,
    )(tokens, cotangent, routes.T, combine.T, hot_experts, extra_slots)
    recv = lax.all_to_all(send, "expert", split_axis=0, concat_axis=0, tiled=True)
    piece = features // ranks
    cut = hidden // 2
    shape = jax.ShapeDtypeStruct
    out = [shape((total, features // 2), BF16)]
    out += [shape((cut, features), BF16)] * 2 + [shape((piece, 2 * hidden), BF16)] * 4
    back, down_a, down_b, even_send, mirror_send, even_keep, mirror_keep = call(
        functools.partial(expert_body, ranks),
        "expert",
        out,
        [SMEM] + [ANY] * 4,
        [pltpu.VMEM(a.shape, a.dtype) for a in out]
        + [
            pltpu.VMEM((total, features), BF16),
            pltpu.VMEM((features, 2 * hidden), BF16),
            pltpu.VMEM((hidden, features), BF16),
            pltpu.VMEM((features // LANES, total, LANES), F32),
            pltpu.VMEM((features // 2 // LANES, total, LANES), F32),
            pltpu.VMEM((rows, features), BF16),
            pltpu.VMEM((rows, features), BF16),
            pltpu.VMEM((rows, 2 * hidden), F32),
            pltpu.VMEM((rows, hidden), F32),
            pltpu.VMEM((rows, 2 * hidden), BF16),
            pltpu.VMEM((rows, hidden), BF16),
            pltpu.VMEM((features, 2 * hidden), F32),
            pltpu.SemaphoreType.DMA((CHUNKS + 3,)),
            pltpu.SemaphoreType.DMA((len(out),)),
        ],
        16 * rows * features * hidden,
        2 * (total * features * 2 + 6 * features * hidden),
        48 * MIB,
        ANY,
    )(me, recv, w_gate[0], w_up[0], w_down[0])
    returned = lax.all_to_all(back, "expert", split_axis=0, concat_axis=0, tiled=True)

    def even(value):
        return lax.ppermute(value, "dp", [(i, i ^ 1) for i in range(ranks)])

    def mirror(value):
        return lax.ppermute(value, "dp", [(i, ranks - 1 - i) for i in range(ranks)])

    def small(body, name, out, *operands):
        moved = sum(2 * a.size for a in operands) + sum(2 * a.size for a in jax.tree.leaves(out))
        return call(
            body, name, out, [VMEM] * len(operands), bytes_accessed=moved
        )(*operands)

    first_a, first_b = even(down_a), mirror(down_b)
    up_first, gate_first = even(even_send), mirror(mirror_send)
    half_down = shape((cut, features), BF16)
    one_piece = shape((piece, hidden), BF16)
    sum_a = small(sum_body, "down_a", half_down, down_a, first_a)
    next_a = mirror(sum_a)
    sum_b = small(sum_body, "down_b", half_down, down_b, first_b)
    next_b = even(sum_b)
    up_next = mirror(small(sum_body, "up", one_piece, even_keep, up_first))
    gate_next = even(small(sum_body, "gate", one_piece, mirror_keep, gate_first))
    grad_down = small(
        down_body, "down", shape((hidden, features), BF16), sum_a, next_a, sum_b, next_b
    )
    grad_gate, grad_up = small(
        pair_body,
        "pair",
        [one_piece, one_piece],
        mirror_keep, gate_first, gate_next, even_keep, up_first, up_next,
    )
    token_grads = call(
        token_body,
        "token_grad",
        jax.ShapeDtypeStruct((count, features), BF16),
        [VMEM, VMEM],
        (),
        2 * total * count * features,
        2 * total * features,
    )(pick_t, returned)
    return token_grads, grad_gate[None], grad_up[None], grad_down[None]


def solution(mesh):
    in_specs = (
        P(("dp", "expert"), None),
        P(("dp", "expert"), None),
        P(("dp", "expert"), None),
        P(("dp", "expert"), None),
        P(),
        P(),
        P("expert", None, None),
        P("expert", None, None),
        P("expert", None, None),
    )
    out_specs = (
        P(("dp", "expert"), None),
        P("expert", "dp", None),
        P("expert", "dp", None),
        P("expert", None, None),
    )
    return jax.shard_map(shards, mesh=mesh, in_specs=in_specs, out_specs=out_specs, check_vma=False)
```

```python
import functools

import jax
import jax.numpy as jnp
from jax import lax
from jax.experimental import pallas as pl
from jax.experimental.pallas import tpu as pltpu
from jax.sharding import PartitionSpec as P

BASE = 2
SLOTS = 4
MSG = 2 * SLOTS
LANES = 128
CHUNKS = 4
EARLY = 10**10
F32 = jnp.float32
BF16 = jnp.bfloat16
VMEM = pl.BlockSpec(memory_space=pltpu.VMEM)
ANY = pl.BlockSpec(memory_space=pl.ANY)
SMEM = pl.BlockSpec(memory_space=pltpu.SMEM)
MIB = 1024 * 1024


NN = (((1,), (0,)), ((), ()))
NT = (((1,), (1,)), ((), ()))
TN = (((0,), (0,)), ((), ()))


def dot(a, b, dims):
    return lax.dot_general(a, b, dims, preferred_element_type=F32)


def call(
    body, name, out_shape, in_specs, scratch=(), flops=0, bytes_accessed=0, vmem=16 * MIB, out=VMEM
):
    return pl.pallas_call(
        body,
        name=name,
        out_shape=out_shape,
        in_specs=in_specs,
        out_specs=jax.tree.map(lambda _: out, out_shape),
        scratch_shapes=list(scratch),
        compiler_params=pltpu.CompilerParams(vmem_limit_bytes=vmem),
        cost_estimate=pl.CostEstimate(
            flops=flops, bytes_accessed=bytes_accessed, transcendentals=0
        ),
    )


def identity(n):
    rows = lax.broadcasted_iota(jnp.int32, (n, n), 0)
    return jnp.where(rows == lax.broadcasted_iota(jnp.int32, (n, n), 1), 1.0, 0.0).astype(BF16)


def dispatch_body(
    experts, tok_hbm, cot_hbm, routes_hbm, combine_hbm, hot_hbm, extra_hbm,
    send_hbm, pick_hbm, send, pick_t, both, routes_in, combine_in, hot, extra, sems, out_sems,
):
    count = tok_hbm.shape[0]
    copies = [
        pltpu.make_async_copy(source, target, sems.at[i])
        for i, (source, target) in enumerate(
            [
                (routes_hbm, routes_in),
                (combine_hbm, combine_in),
                (hot_hbm, hot),
                (extra_hbm, extra),
                (tok_hbm, both.at[pl.ds(0, count)]),
                (cot_hbm, both.at[pl.ds(count, count)]),
            ]
        )
    ]
    for copy in copies:
        copy.start()
    for copy in copies[:4]:
        copy.wait()
    lanes = 2 * count
    src = lax.broadcasted_iota(jnp.int32, (count, lanes), 0)
    dst = lax.broadcasted_iota(jnp.int32, (count, lanes), 1)
    dst = jnp.where(dst >= count, dst - count, dst)
    twice = jnp.where(src == dst, 1.0, 0.0).astype(BF16)
    routes = dot(routes_in[...].astype(F32).astype(BF16), twice, NN)
    combine = dot(combine_in[...], twice, NN)
    expert_id = lax.broadcasted_iota(jnp.int32, (experts, lanes), 0)
    lane = lax.broadcasted_iota(jnp.int32, (experts, lanes), 1)
    named = jnp.zeros((experts, lanes), F32)
    weight = jnp.zeros((experts, lanes), F32)
    expert_number = expert_id.astype(F32)
    for k in range(routes.shape[0]):
        match = expert_number == routes[k : k + 1, :]
        named = named + jnp.where(match, 1.0, 0.0)
        weight = weight + jnp.where(match, combine[k : k + 1, :], 0.0)
    before = jnp.where(src < dst, 1.0, 0.0).astype(BF16)
    rank = dot(named[:, :count].astype(BF16), before, NN)
    limit = jnp.full((experts, lanes), float(BASE), F32)
    for j in range(hot.shape[0]):
        limit = limit + jnp.where(expert_id == hot[j], extra[j].astype(F32), 0.0)
    place = jnp.where(lane >= count, rank + float(SLOTS), rank)
    place = jnp.where(named > 0.5, place, -1.0)
    place = jnp.where(rank < limit, place, -1.0)
    weight = jnp.where(lane >= count, weight, 1.0)
    slot = lax.broadcasted_iota(jnp.int32, (experts, MSG, lanes), 1).astype(F32)
    hit = jnp.broadcast_to(place[:, None, :], (experts, MSG, lanes)) == slot
    scaled = jnp.where(hit, jnp.broadcast_to(weight[:, None, :], hit.shape), 0.0)
    scaled = scaled.reshape(experts * MSG, lanes).astype(BF16)
    for copy in copies[4:]:
        copy.wait()
    part = send.shape[0] // CHUNKS
    departures = []
    for n in range(CHUNKS):
        at = pl.ds(n * part, part)
        block = dot(scaled[n * part : (n + 1) * part, :], both[...], NN)
        send[at, :] = block.astype(BF16)
        departures += start_all([pltpu.make_async_copy(send.at[at], send_hbm.at[at], out_sems.at[n])])
    pick = jnp.where(hit, 1.0, 0.0).reshape(experts * MSG, lanes).astype(BF16)
    pick_t[...] = dot(identity(lanes), pick, NT).astype(BF16)
    departures += start_all([pltpu.make_async_copy(pick_t, pick_hbm, out_sems.at[CHUNKS])])
    wait_all(departures)


def token_body(pick_t, returned, out):
    count, half = out.shape[0], returned.shape[1]
    both = dot(pick_t[...], returned[...], NN)
    out[:, :half] = both[:count].astype(BF16)
    out[:, half:] = both[count:].astype(BF16)


def start_all(copies):
    for copy in copies:
        copy.start()
    return copies


def wait_all(copies):
    for copy in copies:
        copy.wait()


def expert_body(
    ranks, me, recv_hbm, w_gate_hbm, w_up_hbm, w_down_hbm,
    back_hbm, down_a_hbm, down_b_hbm, send_hbm, keep_hbm, back, down_a, down_b, send, keep,
    recv, w_in, w_down, wide, narrow, tok, og, pre, grad, in_rows, hid, total, in_sems, out_sems,
):
    rows_in, features = recv.shape
    hidden = w_down.shape[0]
    peers = rows_in // MSG
    half = features // 2
    step = rows_in // CHUNKS
    chunks = [pl.ds(n * step, step) for n in range(CHUNKS)]
    arrivals = start_all(
        [
            pltpu.make_async_copy(recv_hbm.at[at], recv.at[at], in_sems.at[n])
            for n, at in enumerate(chunks)
        ]
    )
    weights = start_all(
        [
            pltpu.make_async_copy(source, target, in_sems.at[CHUNKS + n])
            for n, (source, target) in enumerate(
                [
                    (w_gate_hbm, w_in.at[:, pl.ds(0, hidden)]),
                    (w_up_hbm, w_in.at[:, pl.ds(hidden, hidden)]),
                    (w_down_hbm, w_down),
                ]
            )
        ]
    )
    departures = []

    def send_out(source, target):
        copy = pltpu.make_async_copy(source, target, out_sems.at[len(departures)])
        departures.extend(start_all([copy]))

    for copy, at in zip(arrivals, chunks):
        copy.wait()
        for c in range(features // LANES):
            wide[c, at, :] = recv[at, c * LANES : (c + 1) * LANES].astype(F32)
    for s in range(SLOTS):
        at = pl.ds(s * peers, peers)
        for c in range(features // LANES):
            cols = slice(c * LANES, (c + 1) * LANES)
            tok[at, cols] = wide[c, pl.ds(s, peers, MSG), :].astype(BF16)
            og[at, cols] = wide[c, pl.ds(s + SLOTS, peers, MSG), :].astype(BF16)
    wait_all(weights)
    pre[...] = dot(tok[...], w_in[...], NN)
    grad[...] = dot(og[...], w_down[...], NT)
    for at in range(0, SLOTS * peers, peers):
        rows = slice(at, at + peers)
        gate_pre, up_proj, hidden_grad = pre[rows, :hidden], pre[rows, hidden:], grad[rows, :]
        s = jax.nn.sigmoid(gate_pre)
        act = gate_pre * s
        hid[rows, :] = (act * up_proj).astype(BF16)
        gate_grad = hidden_grad * up_proj * s * (1.0 + gate_pre * (1.0 - s))
        in_rows[rows, :hidden] = gate_grad.astype(BF16)
        in_rows[rows, hidden:] = (hidden_grad * act).astype(BF16)
    grads = dot(in_rows[...], w_in[...], NT)
    for s in range(SLOTS):
        piece = grads[s * peers : (s + 1) * peers, :]
        for c in range(half // LANES):
            low = piece[:, c * LANES : (c + 1) * LANES]
            high = piece[:, half + c * LANES : half + (c + 1) * LANES]
            narrow[c, pl.ds(s, peers, MSG), :] = low
            narrow[c, pl.ds(s + SLOTS, peers, MSG), :] = high
    for c in range(half // LANES):
        back[:, c * LANES : (c + 1) * LANES] = narrow[c].astype(BF16)
    send_out(back, back_hbm)
    total[...] = dot(tok[...], in_rows[...], TN)
    piece = features // ranks
    even = me[0] + 1 - 2 * lax.rem(me[0], 2)

    def part_of(index):
        return total[pl.ds(pl.multiple_of(index * piece, 16), piece), :].astype(BF16)

    send[:, : 2 * hidden] = part_of(ranks - 1 - even)
    send[:, 2 * hidden :] = part_of(even)
    send_out(send, send_hbm)
    keep[:, : 2 * hidden] = part_of(ranks - 1 - me[0])
    keep[:, 2 * hidden :] = part_of(me[0])
    send_out(keep, keep_hbm)
    down = dot(hid[...], og[...], TN).astype(BF16)
    cut = hidden // 2
    down_a[...] = down[:cut]
    send_out(down_a, down_a_hbm)
    down_b[...] = down[cut:]
    send_out(down_b, down_b_hbm)
    wait_all(departures)


def add(kept, received):
    return kept.astype(F32) + received.astype(F32)


def sum_body(kept, received, out):
    width = out.shape[1]
    out[...] = add(kept[:, :width], received[:, :width]).astype(BF16)


def down_body(sum_a, next_a, sum_b, next_b, out):
    cut = sum_a.shape[0]
    out[:cut, :] = add(sum_a[...], next_a[...]).astype(BF16)
    out[cut:, :] = add(sum_b[...], next_b[...]).astype(BF16)


def pair_body(keep, first, second, grad_gate, grad_up):
    hidden = grad_gate.shape[1]
    own = add(keep[:, 2 * hidden :], first[:, 2 * hidden :]) + second[...].astype(F32)
    grad_gate[...] = own[:, :hidden].astype(BF16)
    grad_up[...] = own[:, hidden:].astype(BF16)


def shards(tokens, cotangent, routes, combine, hot_experts, extra_slots, w_gate, w_up, w_down):
    experts = lax.axis_size("expert")
    ranks = lax.axis_size("dp")
    count, features = tokens.shape
    hidden = w_gate.shape[2]
    total = experts * MSG
    rows = experts * SLOTS
    me = lax.axis_index("dp").astype(jnp.int32).reshape(1)
    me, hot_experts = lax.optimization_barrier((me, hot_experts))
    send, pick_t = call(
        functools.partial(dispatch_body, experts),
        "dispatch",
        [
            jax.ShapeDtypeStruct((total, features), BF16),
            jax.ShapeDtypeStruct((2 * count, total), BF16),
        ],
        [ANY] * 6,
        [
            pltpu.VMEM((total, features), BF16),
            pltpu.VMEM((2 * count, total), BF16),
            pltpu.VMEM((2 * count, features), BF16),
            pltpu.VMEM(routes.shape[::-1], jnp.int32),
            pltpu.VMEM(combine.shape[::-1], BF16),
            pltpu.SMEM(hot_experts.shape, jnp.int32),
            pltpu.SMEM(extra_slots.shape, jnp.int32),
            pltpu.SemaphoreType.DMA((6,)),
            pltpu.SemaphoreType.DMA((CHUNKS + 1,)),
        ],
        2 * total * 2 * count * features,
        2 * total * features,
        64 * MIB - 65536,
        ANY,
    )(tokens, cotangent, routes.T, combine.T, hot_experts, extra_slots)
    recv = lax.all_to_all(send, "expert", split_axis=0, concat_axis=0, tiled=True)
    piece = features // ranks
    cut = hidden // 2
    shape = jax.ShapeDtypeStruct
    out = [shape((total, features // 2), BF16)]
    out += [shape((cut, features), BF16)] * 2 + [shape((piece, 4 * hidden), BF16)] * 2
    back, down_a, down_b, send, keep = call(
        functools.partial(expert_body, ranks),
        "expert",
        out,
        [SMEM] + [ANY] * 4,
        [pltpu.VMEM(a.shape, a.dtype) for a in out]
        + [
            pltpu.VMEM((total, features), BF16),
            pltpu.VMEM((features, 2 * hidden), BF16),
            pltpu.VMEM((hidden, features), BF16),
            pltpu.VMEM((features // LANES, total, LANES), F32),
            pltpu.VMEM((features // 2 // LANES, total, LANES), F32),
            pltpu.VMEM((rows, features), BF16),
            pltpu.VMEM((rows, features), BF16),
            pltpu.VMEM((rows, 2 * hidden), F32),
            pltpu.VMEM((rows, hidden), F32),
            pltpu.VMEM((rows, 2 * hidden), BF16),
            pltpu.VMEM((rows, hidden), BF16),
            pltpu.VMEM((features, 2 * hidden), F32),
            pltpu.SemaphoreType.DMA((CHUNKS + 3,)),
            pltpu.SemaphoreType.DMA((len(out),)),
        ],
        16 * rows * features * hidden,
        2 * (total * features * 2 + 6 * features * hidden),
        44 * MIB,
        ANY,
    )(me, recv, w_gate[0], w_up[0], w_down[0])
    returned = lax.all_to_all(back, "expert", split_axis=0, concat_axis=0, tiled=True)

    def even(value):
        return lax.ppermute(value, "dp", [(i, i ^ 1) for i in range(ranks)])

    def mirror(value):
        return lax.ppermute(value, "dp", [(i, ranks - 1 - i) for i in range(ranks)])

    def small(body, name, out, *operands, work=0):
        moved = sum(2 * a.size for a in operands) + sum(2 * a.size for a in jax.tree.leaves(out))
        return call(
            body, name, out, [VMEM] * len(operands), flops=work, bytes_accessed=moved
        )(*operands)

    half_down = shape((cut, features), BF16)
    one_piece = shape((piece, hidden), BF16)
    first = even(send)
    first_b = mirror(down_b)
    first_a = even(down_a)
    both_pieces = shape((piece, 2 * hidden), BF16)
    sum_b = small(sum_body, "down_b", half_down, down_b, first_b)
    next_b = even(sum_b)
    pair_sum = small(sum_body, "pair_sum", both_pieces, keep, first, work=EARLY)
    second = mirror(pair_sum)
    kept_a, _, _ = lax.optimization_barrier((down_a, sum_b, pair_sum))
    sum_a = small(sum_body, "down_a", half_down, kept_a, first_a)
    next_a = mirror(sum_a)
    grad_down = small(
        down_body, "down", shape((hidden, features), BF16), sum_a, next_a, sum_b, next_b
    )
    grad_gate, grad_up = small(pair_body, "pair", [one_piece, one_piece], keep, first, second)
    token_grads = call(
        token_body,
        "token_grad",
        jax.ShapeDtypeStruct((count, features), BF16),
        [VMEM, VMEM],
        (),
        2 * total * count * features,
        2 * total * features,
    )(pick_t, returned)
    return token_grads, grad_gate[None], grad_up[None], grad_down[None]


def solution(mesh):
    in_specs = (
        P(("dp", "expert"), None),
        P(("dp", "expert"), None),
        P(("dp", "expert"), None),
        P(("dp", "expert"), None),
        P(),
        P(),
        P("expert", None, None),
        P("expert", None, None),
        P("expert", None, None),
    )
    out_specs = (
        P(("dp", "expert"), None),
        P("expert", "dp", None),
        P("expert", "dp", None),
        P("expert", None, None),
    )
    return jax.shard_map(shards, mesh=mesh, in_specs=in_specs, out_specs=out_specs, check_vma=False)
```

```python
import functools

import jax
import jax.numpy as jnp
from jax import lax
from jax.experimental import pallas as pl
from jax.experimental.pallas import tpu as pltpu
from jax.sharding import PartitionSpec as P

BASE = 2
SLOTS = 4
MSG = 2 * SLOTS
LANES = 128
CHUNKS = 4
EARLY = 3 * 10**10
F32 = jnp.float32
BF16 = jnp.bfloat16
VMEM = pl.BlockSpec(memory_space=pltpu.VMEM)
ANY = pl.BlockSpec(memory_space=pl.ANY)
SMEM = pl.BlockSpec(memory_space=pltpu.SMEM)
MIB = 1024 * 1024


NN = (((1,), (0,)), ((), ()))
NT = (((1,), (1,)), ((), ()))
TN = (((0,), (0,)), ((), ()))


def dot(a, b, dims):
    return lax.dot_general(a, b, dims, preferred_element_type=F32)


def call(
    body, name, out_shape, in_specs, scratch=(), flops=0, bytes_accessed=0, vmem=16 * MIB, out=VMEM
):
    return pl.pallas_call(
        body,
        name=name,
        out_shape=out_shape,
        in_specs=in_specs,
        out_specs=jax.tree.map(lambda _: out, out_shape),
        scratch_shapes=list(scratch),
        compiler_params=pltpu.CompilerParams(vmem_limit_bytes=vmem),
        cost_estimate=pl.CostEstimate(
            flops=flops, bytes_accessed=bytes_accessed, transcendentals=0
        ),
    )


def identity(n):
    rows = lax.broadcasted_iota(jnp.int32, (n, n), 0)
    return jnp.where(rows == lax.broadcasted_iota(jnp.int32, (n, n), 1), 1.0, 0.0).astype(BF16)


def dispatch_body(
    experts, tok_hbm, cot_hbm, routes_hbm, combine_hbm, hot_hbm, extra_hbm,
    send_hbm, pick_hbm, send, pick_t, both, routes_in, combine_in, hot, extra, sems, out_sems,
):
    count = tok_hbm.shape[0]
    copies = [
        pltpu.make_async_copy(source, target, sems.at[i])
        for i, (source, target) in enumerate(
            [
                (routes_hbm, routes_in),
                (combine_hbm, combine_in),
                (hot_hbm, hot),
                (extra_hbm, extra),
                (tok_hbm, both.at[pl.ds(0, count)]),
                (cot_hbm, both.at[pl.ds(count, count)]),
            ]
        )
    ]
    for copy in copies:
        copy.start()
    for copy in copies[:4]:
        copy.wait()
    lanes = 2 * count
    src = lax.broadcasted_iota(jnp.int32, (count, lanes), 0)
    dst = lax.broadcasted_iota(jnp.int32, (count, lanes), 1)
    dst = jnp.where(dst >= count, dst - count, dst)
    twice = jnp.where(src == dst, 1.0, 0.0).astype(BF16)
    routes = dot(routes_in[...].astype(F32).astype(BF16), twice, NN)
    combine = dot(combine_in[...], twice, NN)
    expert_id = lax.broadcasted_iota(jnp.int32, (experts, lanes), 0)
    lane = lax.broadcasted_iota(jnp.int32, (experts, lanes), 1)
    named = jnp.zeros((experts, lanes), F32)
    weight = jnp.zeros((experts, lanes), F32)
    expert_number = expert_id.astype(F32)
    for k in range(routes.shape[0]):
        match = expert_number == routes[k : k + 1, :]
        named = named + jnp.where(match, 1.0, 0.0)
        weight = weight + jnp.where(match, combine[k : k + 1, :], 0.0)
    before = jnp.where(src < dst, 1.0, 0.0).astype(BF16)
    rank = dot(named[:, :count].astype(BF16), before, NN)
    limit = jnp.full((experts, lanes), float(BASE), F32)
    for j in range(hot.shape[0]):
        limit = limit + jnp.where(expert_id == hot[j], extra[j].astype(F32), 0.0)
    place = jnp.where(lane >= count, rank + float(SLOTS), rank)
    place = jnp.where(named > 0.5, place, -1.0)
    place = jnp.where(rank < limit, place, -1.0)
    weight = jnp.where(lane >= count, weight, 1.0)
    slot = lax.broadcasted_iota(jnp.int32, (experts, MSG, lanes), 1).astype(F32)
    hit = jnp.broadcast_to(place[:, None, :], (experts, MSG, lanes)) == slot
    scaled = jnp.where(hit, jnp.broadcast_to(weight[:, None, :], hit.shape), 0.0)
    scaled = scaled.reshape(experts * MSG, lanes).astype(BF16)
    for copy in copies[4:]:
        copy.wait()
    part = send.shape[0] // CHUNKS
    departures = []
    for n in range(CHUNKS):
        at = pl.ds(n * part, part)
        block = dot(scaled[n * part : (n + 1) * part, :], both[...], NN)
        send[at, :] = block.astype(BF16)
        departures += start_all([pltpu.make_async_copy(send.at[at], send_hbm.at[at], out_sems.at[n])])
    pick = jnp.where(hit, 1.0, 0.0).reshape(experts * MSG, lanes).astype(BF16)
    pick_t[...] = dot(identity(lanes), pick, NT).astype(BF16)
    departures += start_all([pltpu.make_async_copy(pick_t, pick_hbm, out_sems.at[CHUNKS])])
    wait_all(departures)


def token_body(pick_t, returned, out):
    count, half = out.shape[0], returned.shape[1]
    both = dot(pick_t[...], returned[...], NN)
    out[:, :half] = both[:count].astype(BF16)
    out[:, half:] = both[count:].astype(BF16)


def start_all(copies):
    for copy in copies:
        copy.start()
    return copies


def wait_all(copies):
    for copy in copies:
        copy.wait()


def expert_body(
    ranks, me, recv_hbm, w_gate_hbm, w_up_hbm, w_down_hbm,
    back_hbm, down_a_hbm, down_b_hbm, send_hbm, keep_hbm, back, down_a, down_b, send, keep,
    recv, w_in, w_down, wide, narrow, tok, og, pre, grad, in_rows, hid, total, in_sems, out_sems,
):
    rows_in, features = recv.shape
    hidden = w_down.shape[0]
    peers = rows_in // MSG
    half = features // 2
    step = rows_in // CHUNKS
    chunks = [pl.ds(n * step, step) for n in range(CHUNKS)]
    arrivals = start_all(
        [
            pltpu.make_async_copy(recv_hbm.at[at], recv.at[at], in_sems.at[n])
            for n, at in enumerate(chunks)
        ]
    )
    weights = start_all(
        [
            pltpu.make_async_copy(source, target, in_sems.at[CHUNKS + n])
            for n, (source, target) in enumerate(
                [
                    (w_gate_hbm, w_in.at[:, pl.ds(0, hidden)]),
                    (w_up_hbm, w_in.at[:, pl.ds(hidden, hidden)]),
                    (w_down_hbm, w_down),
                ]
            )
        ]
    )
    departures = []

    def send_out(source, target):
        copy = pltpu.make_async_copy(source, target, out_sems.at[len(departures)])
        departures.extend(start_all([copy]))

    for copy, at in zip(arrivals, chunks):
        copy.wait()
        for c in range(features // LANES):
            wide[c, at, :] = recv[at, c * LANES : (c + 1) * LANES].astype(F32)
    for s in range(SLOTS):
        at = pl.ds(s * peers, peers)
        for c in range(features // LANES):
            cols = slice(c * LANES, (c + 1) * LANES)
            tok[at, cols] = wide[c, pl.ds(s, peers, MSG), :].astype(BF16)
            og[at, cols] = wide[c, pl.ds(s + SLOTS, peers, MSG), :].astype(BF16)
    wait_all(weights)
    pre[...] = dot(tok[...], w_in[...], NN)
    grad[...] = dot(og[...], w_down[...], NT)
    for at in range(0, SLOTS * peers, peers):
        rows = slice(at, at + peers)
        gate_pre, up_proj, hidden_grad = pre[rows, :hidden], pre[rows, hidden:], grad[rows, :]
        s = jax.nn.sigmoid(gate_pre)
        act = gate_pre * s
        hid[rows, :] = (act * up_proj).astype(BF16)
        gate_grad = hidden_grad * up_proj * s * (1.0 + gate_pre * (1.0 - s))
        in_rows[rows, :hidden] = gate_grad.astype(BF16)
        in_rows[rows, hidden:] = (hidden_grad * act).astype(BF16)
    grads = dot(in_rows[...], w_in[...], NT)
    for s in range(SLOTS):
        piece = grads[s * peers : (s + 1) * peers, :]
        for c in range(half // LANES):
            low = piece[:, c * LANES : (c + 1) * LANES]
            high = piece[:, half + c * LANES : half + (c + 1) * LANES]
            narrow[c, pl.ds(s, peers, MSG), :] = low
            narrow[c, pl.ds(s + SLOTS, peers, MSG), :] = high
    for c in range(half // LANES):
        back[:, c * LANES : (c + 1) * LANES] = narrow[c].astype(BF16)
    send_out(back, back_hbm)
    total[...] = dot(tok[...], in_rows[...], TN)
    piece = features // ranks
    even = me[0] + 1 - 2 * lax.rem(me[0], 2)

    def part_of(index):
        return total[pl.ds(pl.multiple_of(index * piece, 16), piece), :].astype(BF16)

    send[:, : 2 * hidden] = part_of(ranks - 1 - even)
    send[:, 2 * hidden :] = part_of(even)
    send_out(send, send_hbm)
    keep[:, : 2 * hidden] = part_of(ranks - 1 - me[0])
    keep[:, 2 * hidden :] = part_of(me[0])
    send_out(keep, keep_hbm)
    down = dot(hid[...], og[...], TN).astype(BF16)
    cut = down_a.shape[0]
    down_a[...] = down[:cut]
    send_out(down_a, down_a_hbm)
    down_b[...] = down[cut:]
    send_out(down_b, down_b_hbm)
    wait_all(departures)


def add(kept, received):
    return kept.astype(F32) + received.astype(F32)


def sum_body(kept, received, out):
    width = out.shape[1]
    out[...] = add(kept[:, :width], received[:, :width]).astype(BF16)


def down_body(sum_a, next_a, sum_b, next_b, out):
    cut = sum_a.shape[0]
    out[:cut, :] = add(sum_a[...], next_a[...]).astype(BF16)
    out[cut:, :] = add(sum_b[...], next_b[...]).astype(BF16)


def pair_body(keep, first, second, grad_gate, grad_up):
    hidden = grad_gate.shape[1]
    own = add(keep[:, 2 * hidden :], first[:, 2 * hidden :]) + second[...].astype(F32)
    grad_gate[...] = own[:, :hidden].astype(BF16)
    grad_up[...] = own[:, hidden:].astype(BF16)


def shards(tokens, cotangent, routes, combine, hot_experts, extra_slots, w_gate, w_up, w_down):
    experts = lax.axis_size("expert")
    ranks = lax.axis_size("dp")
    count, features = tokens.shape
    hidden = w_gate.shape[2]
    total = experts * MSG
    rows = experts * SLOTS
    me = lax.axis_index("dp").astype(jnp.int32).reshape(1)
    me, hot_experts = lax.optimization_barrier((me, hot_experts))
    send, pick_t = call(
        functools.partial(dispatch_body, experts),
        "dispatch",
        [
            jax.ShapeDtypeStruct((total, features), BF16),
            jax.ShapeDtypeStruct((2 * count, total), BF16),
        ],
        [ANY] * 6,
        [
            pltpu.VMEM((total, features), BF16),
            pltpu.VMEM((2 * count, total), BF16),
            pltpu.VMEM((2 * count, features), BF16),
            pltpu.VMEM(routes.shape[::-1], jnp.int32),
            pltpu.VMEM(combine.shape[::-1], BF16),
            pltpu.SMEM(hot_experts.shape, jnp.int32),
            pltpu.SMEM(extra_slots.shape, jnp.int32),
            pltpu.SemaphoreType.DMA((6,)),
            pltpu.SemaphoreType.DMA((CHUNKS + 1,)),
        ],
        2 * total * 2 * count * features,
        2 * total * features,
        64 * MIB - 65536,
        ANY,
    )(tokens, cotangent, routes.T, combine.T, hot_experts, extra_slots)
    recv = lax.all_to_all(send, "expert", split_axis=0, concat_axis=0, tiled=True)
    piece = features // ranks
    cut = hidden // 3
    shape = jax.ShapeDtypeStruct
    out = [shape((total, features // 2), BF16)]
    parts = [shape((cut, features), BF16), shape((hidden - cut, features), BF16)]
    out += parts + [shape((piece, 4 * hidden), BF16)] * 2
    back, down_a, down_b, send, keep = call(
        functools.partial(expert_body, ranks),
        "expert",
        out,
        [SMEM] + [ANY] * 4,
        [pltpu.VMEM(a.shape, a.dtype) for a in out]
        + [
            pltpu.VMEM((total, features), BF16),
            pltpu.VMEM((features, 2 * hidden), BF16),
            pltpu.VMEM((hidden, features), BF16),
            pltpu.VMEM((features // LANES, total, LANES), F32),
            pltpu.VMEM((features // 2 // LANES, total, LANES), F32),
            pltpu.VMEM((rows, features), BF16),
            pltpu.VMEM((rows, features), BF16),
            pltpu.VMEM((rows, 2 * hidden), F32),
            pltpu.VMEM((rows, hidden), F32),
            pltpu.VMEM((rows, 2 * hidden), BF16),
            pltpu.VMEM((rows, hidden), BF16),
            pltpu.VMEM((features, 2 * hidden), F32),
            pltpu.SemaphoreType.DMA((CHUNKS + 3,)),
            pltpu.SemaphoreType.DMA((len(out),)),
        ],
        16 * rows * features * hidden,
        2 * (total * features * 2 + 6 * features * hidden),
        44 * MIB,
        ANY,
    )(me, recv, w_gate[0], w_up[0], w_down[0])
    returned = lax.all_to_all(back, "expert", split_axis=0, concat_axis=0, tiled=True)

    def even(value):
        return lax.ppermute(value, "dp", [(i, i ^ 1) for i in range(ranks)])

    def mirror(value):
        return lax.ppermute(value, "dp", [(i, ranks - 1 - i) for i in range(ranks)])

    def small(body, name, out, *operands, work=0):
        moved = sum(2 * a.size for a in operands) + sum(2 * a.size for a in jax.tree.leaves(out))
        return call(
            body, name, out, [VMEM] * len(operands), flops=work, bytes_accessed=moved
        )(*operands)

    one_piece = shape((piece, hidden), BF16)
    first = even(send)
    first_b = mirror(down_b)
    first_a = even(down_a)
    both_pieces = shape((piece, 2 * hidden), BF16)
    sum_b = small(sum_body, "down_b", parts[1], down_b, first_b)
    next_b = even(sum_b)
    pair_sum = small(sum_body, "pair_sum", both_pieces, keep, first, work=EARLY)
    second = mirror(pair_sum)
    kept_a, _, _ = lax.optimization_barrier((down_a, sum_b, pair_sum))
    sum_a = small(sum_body, "down_a", parts[0], kept_a, first_a)
    next_a = mirror(sum_a)
    grad_down = small(
        down_body, "down", shape((hidden, features), BF16), sum_a, next_a, sum_b, next_b
    )
    grad_gate, grad_up = small(pair_body, "pair", [one_piece, one_piece], keep, first, second)
    token_grads = call(
        token_body,
        "token_grad",
        jax.ShapeDtypeStruct((count, features), BF16),
        [VMEM, VMEM],
        (),
        2 * total * count * features,
        2 * total * features,
    )(pick_t, returned)
    return token_grads, grad_gate[None], grad_up[None], grad_down[None]


def solution(mesh):
    in_specs = (
        P(("dp", "expert"), None),
        P(("dp", "expert"), None),
        P(("dp", "expert"), None),
        P(("dp", "expert"), None),
        P(),
        P(),
        P("expert", None, None),
        P("expert", None, None),
        P("expert", None, None),
    )
    out_specs = (
        P(("dp", "expert"), None),
        P("expert", "dp", None),
        P("expert", "dp", None),
        P("expert", None, None),
    )
    return jax.shard_map(shards, mesh=mesh, in_specs=in_specs, out_specs=out_specs, check_vma=False)
```

```python
import functools

import jax
import jax.numpy as jnp
from jax import lax
from jax.experimental import pallas as pl
from jax.experimental.pallas import tpu as pltpu
from jax.sharding import PartitionSpec as P

BASE = 2
SLOTS = 4
MSG = 2 * SLOTS
LANES = 128
CHUNKS = 4
LATER = 10**10
SOONER = 5 * 10**9
F32 = jnp.float32
BF16 = jnp.bfloat16
VMEM = pl.BlockSpec(memory_space=pltpu.VMEM)
ANY = pl.BlockSpec(memory_space=pl.ANY)
SMEM = pl.BlockSpec(memory_space=pltpu.SMEM)
MIB = 1024 * 1024


NN = (((1,), (0,)), ((), ()))
NT = (((1,), (1,)), ((), ()))
TN = (((0,), (0,)), ((), ()))


def dot(a, b, dims):
    return lax.dot_general(a, b, dims, preferred_element_type=F32)


def call(
    body, name, out_shape, in_specs, scratch=(), flops=0, bytes_accessed=0, vmem=16 * MIB, out=VMEM
):
    return pl.pallas_call(
        body,
        name=name,
        out_shape=out_shape,
        in_specs=in_specs,
        out_specs=jax.tree.map(lambda _: out, out_shape),
        scratch_shapes=list(scratch),
        compiler_params=pltpu.CompilerParams(vmem_limit_bytes=vmem),
        cost_estimate=pl.CostEstimate(
            flops=flops, bytes_accessed=bytes_accessed, transcendentals=0
        ),
    )


def identity(n):
    rows = lax.broadcasted_iota(jnp.int32, (n, n), 0)
    return jnp.where(rows == lax.broadcasted_iota(jnp.int32, (n, n), 1), 1.0, 0.0).astype(BF16)


def dispatch_body(
    experts, tok_hbm, cot_hbm, routes_hbm, combine_hbm, hot_hbm, extra_hbm,
    send_hbm, pick_hbm, send, pick_t, both, routes_in, combine_in, hot, extra, sems, out_sems,
):
    count = tok_hbm.shape[0]
    copies = [
        pltpu.make_async_copy(source, target, sems.at[i])
        for i, (source, target) in enumerate(
            [
                (routes_hbm, routes_in),
                (combine_hbm, combine_in),
                (hot_hbm, hot),
                (extra_hbm, extra),
                (tok_hbm, both.at[pl.ds(0, count)]),
                (cot_hbm, both.at[pl.ds(count, count)]),
            ]
        )
    ]
    for copy in copies:
        copy.start()
    for copy in copies[:4]:
        copy.wait()
    lanes = 2 * count
    src = lax.broadcasted_iota(jnp.int32, (count, lanes), 0)
    dst = lax.broadcasted_iota(jnp.int32, (count, lanes), 1)
    dst = jnp.where(dst >= count, dst - count, dst)
    twice = jnp.where(src == dst, 1.0, 0.0).astype(BF16)
    routes = dot(routes_in[...].astype(F32).astype(BF16), twice, NN)
    combine = dot(combine_in[...], twice, NN)
    expert_id = lax.broadcasted_iota(jnp.int32, (experts, lanes), 0)
    lane = lax.broadcasted_iota(jnp.int32, (experts, lanes), 1)
    named = jnp.zeros((experts, lanes), F32)
    weight = jnp.zeros((experts, lanes), F32)
    expert_number = expert_id.astype(F32)
    for k in range(routes.shape[0]):
        match = expert_number == routes[k : k + 1, :]
        named = named + jnp.where(match, 1.0, 0.0)
        weight = weight + jnp.where(match, combine[k : k + 1, :], 0.0)
    before = jnp.where(src < dst, 1.0, 0.0).astype(BF16)
    rank = dot(named[:, :count].astype(BF16), before, NN)
    limit = jnp.full((experts, lanes), float(BASE), F32)
    for j in range(hot.shape[0]):
        limit = limit + jnp.where(expert_id == hot[j], extra[j].astype(F32), 0.0)
    place = jnp.where(lane >= count, rank + float(SLOTS), rank)
    place = jnp.where(named > 0.5, place, -1.0)
    place = jnp.where(rank < limit, place, -1.0)
    weight = jnp.where(lane >= count, weight, 1.0)
    slot = lax.broadcasted_iota(jnp.int32, (experts, MSG, lanes), 1).astype(F32)
    hit = jnp.broadcast_to(place[:, None, :], (experts, MSG, lanes)) == slot
    scaled = jnp.where(hit, jnp.broadcast_to(weight[:, None, :], hit.shape), 0.0)
    scaled = scaled.reshape(experts * MSG, lanes).astype(BF16)
    for copy in copies[4:]:
        copy.wait()
    part = send.shape[0] // CHUNKS
    departures = []
    for n in range(CHUNKS):
        at = pl.ds(n * part, part)
        block = dot(scaled[n * part : (n + 1) * part, :], both[...], NN)
        send[at, :] = block.astype(BF16)
        departures += start_all([pltpu.make_async_copy(send.at[at], send_hbm.at[at], out_sems.at[n])])
    pick = jnp.where(hit, 1.0, 0.0).reshape(experts * MSG, lanes).astype(BF16)
    pick_t[...] = dot(identity(lanes), pick, NT).astype(BF16)
    departures += start_all([pltpu.make_async_copy(pick_t, pick_hbm, out_sems.at[CHUNKS])])
    wait_all(departures)


def token_body(pick_t, returned, out):
    count, half = out.shape[0], returned.shape[1]
    both = dot(pick_t[...], returned[...], NN)
    out[:, :half] = both[:count].astype(BF16)
    out[:, half:] = both[count:].astype(BF16)


def start_all(copies):
    for copy in copies:
        copy.start()
    return copies


def wait_all(copies):
    for copy in copies:
        copy.wait()


def expert_body(
    ranks, me, recv, w_gate_hbm, w_up_hbm, w_down_hbm,
    back_hbm, down_a_hbm, down_b_hbm, send_hbm, keep_hbm, back, down_a, down_b, send, keep,
    w_in, w_down, wide, narrow, tok, og, pre, grad, in_rows, hid, total, in_sems, out_sems,
):
    rows_in, features = recv.shape
    hidden = w_down.shape[0]
    peers = rows_in // MSG
    half = features // 2
    weights = start_all(
        [
            pltpu.make_async_copy(source, target, in_sems.at[n])
            for n, (source, target) in enumerate(
                [
                    (w_gate_hbm, w_in.at[:, pl.ds(0, hidden)]),
                    (w_up_hbm, w_in.at[:, pl.ds(hidden, hidden)]),
                    (w_down_hbm, w_down),
                ]
            )
        ]
    )
    departures = []

    def send_out(source, target):
        copy = pltpu.make_async_copy(source, target, out_sems.at[len(departures)])
        departures.extend(start_all([copy]))

    for c in range(features // LANES):
        wide[c] = recv[:, c * LANES : (c + 1) * LANES].astype(F32)
    for s in range(SLOTS):
        at = pl.ds(s * peers, peers)
        for c in range(features // LANES):
            cols = slice(c * LANES, (c + 1) * LANES)
            tok[at, cols] = wide[c, pl.ds(s, peers, MSG), :].astype(BF16)
            og[at, cols] = wide[c, pl.ds(s + SLOTS, peers, MSG), :].astype(BF16)
    wait_all(weights)
    pre[...] = dot(tok[...], w_in[...], NN)
    grad[...] = dot(og[...], w_down[...], NT)
    for at in range(0, SLOTS * peers, peers):
        rows = slice(at, at + peers)
        gate_pre, up_proj, hidden_grad = pre[rows, :hidden], pre[rows, hidden:], grad[rows, :]
        s = jax.nn.sigmoid(gate_pre)
        act = gate_pre * s
        hid[rows, :] = (act * up_proj).astype(BF16)
        gate_grad = hidden_grad * up_proj * s * (1.0 + gate_pre * (1.0 - s))
        in_rows[rows, :hidden] = gate_grad.astype(BF16)
        in_rows[rows, hidden:] = (hidden_grad * act).astype(BF16)
    grads = dot(in_rows[...], w_in[...], NT)
    for s in range(SLOTS):
        piece = grads[s * peers : (s + 1) * peers, :]
        for c in range(half // LANES):
            low = piece[:, c * LANES : (c + 1) * LANES]
            high = piece[:, half + c * LANES : half + (c + 1) * LANES]
            narrow[c, pl.ds(s, peers, MSG), :] = low
            narrow[c, pl.ds(s + SLOTS, peers, MSG), :] = high
    for c in range(half // LANES):
        back[:, c * LANES : (c + 1) * LANES] = narrow[c].astype(BF16)
    send_out(back, back_hbm)
    total[...] = dot(tok[...], in_rows[...], TN)
    piece = features // ranks
    even = me[0] + 1 - 2 * lax.rem(me[0], 2)

    def part_of(index):
        return total[pl.ds(pl.multiple_of(index * piece, 16), piece), :].astype(BF16)

    send[:, : 2 * hidden] = part_of(ranks - 1 - even)
    send[:, 2 * hidden :] = part_of(even)
    send_out(send, send_hbm)
    keep[:, : 2 * hidden] = part_of(ranks - 1 - me[0])
    keep[:, 2 * hidden :] = part_of(me[0])
    send_out(keep, keep_hbm)
    down = dot(hid[...], og[...], TN).astype(BF16)
    cut = down_a.shape[0]
    down_a[...] = down[:cut]
    send_out(down_a, down_a_hbm)
    down_b[...] = down[cut:]
    send_out(down_b, down_b_hbm)
    wait_all(departures)


def add(kept, received):
    return kept.astype(F32) + received.astype(F32)


def sum_body(kept, received, out):
    width = out.shape[1]
    out[...] = add(kept[:, :width], received[:, :width]).astype(BF16)


def down_body(sum_a, next_a, sum_b, next_b, out):
    cut = sum_a.shape[0]
    out[:cut, :] = add(sum_a[...], next_a[...]).astype(BF16)
    out[cut:, :] = add(sum_b[...], next_b[...]).astype(BF16)


def pair_body(keep, first, second, grad_gate, grad_up):
    hidden = grad_gate.shape[1]
    own = add(keep[:, 2 * hidden :], first[:, 2 * hidden :]) + second[...].astype(F32)
    grad_gate[...] = own[:, :hidden].astype(BF16)
    grad_up[...] = own[:, hidden:].astype(BF16)


def shards(tokens, cotangent, routes, combine, hot_experts, extra_slots, w_gate, w_up, w_down):
    experts = lax.axis_size("expert")
    ranks = lax.axis_size("dp")
    count, features = tokens.shape
    hidden = w_gate.shape[2]
    total = experts * MSG
    rows = experts * SLOTS
    me = lax.axis_index("dp").astype(jnp.int32).reshape(1)
    me, hot_experts = lax.optimization_barrier((me, hot_experts))
    send, pick_t = call(
        functools.partial(dispatch_body, experts),
        "dispatch",
        [
            jax.ShapeDtypeStruct((total, features), BF16),
            jax.ShapeDtypeStruct((2 * count, total), BF16),
        ],
        [ANY] * 6,
        [
            pltpu.VMEM((total, features), BF16),
            pltpu.VMEM((2 * count, total), BF16),
            pltpu.VMEM((2 * count, features), BF16),
            pltpu.VMEM(routes.shape[::-1], jnp.int32),
            pltpu.VMEM(combine.shape[::-1], BF16),
            pltpu.SMEM(hot_experts.shape, jnp.int32),
            pltpu.SMEM(extra_slots.shape, jnp.int32),
            pltpu.SemaphoreType.DMA((6,)),
            pltpu.SemaphoreType.DMA((CHUNKS + 1,)),
        ],
        2 * total * 2 * count * features,
        2 * total * features,
        64 * MIB - 65536,
        ANY,
    )(tokens, cotangent, routes.T, combine.T, hot_experts, extra_slots)
    recv = lax.all_to_all(send, "expert", split_axis=0, concat_axis=0, tiled=True)
    piece = features // ranks
    cut = hidden // 3
    shape = jax.ShapeDtypeStruct
    out = [shape((total, features // 2), BF16)]
    parts = [shape((cut, features), BF16), shape((hidden - cut, features), BF16)]
    out += parts + [shape((piece, 4 * hidden), BF16)] * 2
    back, down_a, down_b, send, keep = call(
        functools.partial(expert_body, ranks),
        "expert",
        out,
        [SMEM, VMEM] + [ANY] * 3,
        [pltpu.VMEM(a.shape, a.dtype) for a in out]
        + [
            pltpu.VMEM((features, 2 * hidden), BF16),
            pltpu.VMEM((hidden, features), BF16),
            pltpu.VMEM((features // LANES, total, LANES), F32),
            pltpu.VMEM((features // 2 // LANES, total, LANES), F32),
            pltpu.VMEM((rows, features), BF16),
            pltpu.VMEM((rows, features), BF16),
            pltpu.VMEM((rows, 2 * hidden), F32),
            pltpu.VMEM((rows, hidden), F32),
            pltpu.VMEM((rows, 2 * hidden), BF16),
            pltpu.VMEM((rows, hidden), BF16),
            pltpu.VMEM((features, 2 * hidden), F32),
            pltpu.SemaphoreType.DMA((3,)),
            pltpu.SemaphoreType.DMA((len(out),)),
        ],
        16 * rows * features * hidden,
        2 * (total * features * 2 + 6 * features * hidden),
        44 * MIB,
        ANY,
    )(me, recv, w_gate[0], w_up[0], w_down[0])
    returned = lax.all_to_all(back, "expert", split_axis=0, concat_axis=0, tiled=True)

    def even(value):
        return lax.ppermute(value, "dp", [(i, i ^ 1) for i in range(ranks)])

    def mirror(value):
        return lax.ppermute(value, "dp", [(i, ranks - 1 - i) for i in range(ranks)])

    def small(body, name, out, *operands, work=0):
        moved = sum(2 * a.size for a in operands) + sum(2 * a.size for a in jax.tree.leaves(out))
        return call(
            body, name, out, [VMEM] * len(operands), flops=work, bytes_accessed=moved
        )(*operands)

    one_piece = shape((piece, hidden), BF16)
    first = even(send)
    first_b = mirror(down_b)
    first_a = even(down_a)
    both_pieces = shape((piece, 2 * hidden), BF16)
    sum_b = small(sum_body, "down_b", parts[1], down_b, first_b, work=SOONER)
    next_b = even(sum_b)
    pair_sum = small(sum_body, "pair_sum", both_pieces, keep, first, work=LATER)
    second = mirror(pair_sum)
    kept_a, _, _ = lax.optimization_barrier((down_a, sum_b, pair_sum))
    sum_a = small(sum_body, "down_a", parts[0], kept_a, first_a, work=LATER)
    next_a = mirror(sum_a)
    grad_down = small(
        down_body, "down", shape((hidden, features), BF16), sum_a, next_a, sum_b, next_b
    )
    grad_gate, grad_up = small(pair_body, "pair", [one_piece, one_piece], keep, first, second)
    token_grads = call(
        token_body,
        "token_grad",
        jax.ShapeDtypeStruct((count, features), BF16),
        [VMEM, VMEM],
        (),
        2 * total * count * features,
        2 * total * features,
    )(pick_t, returned)
    return token_grads, grad_gate[None], grad_up[None], grad_down[None]


def solution(mesh):
    in_specs = (
        P(("dp", "expert"), None),
        P(("dp", "expert"), None),
        P(("dp", "expert"), None),
        P(("dp", "expert"), None),
        P(),
        P(),
        P("expert", None, None),
        P("expert", None, None),
        P("expert", None, None),
    )
    out_specs = (
        P(("dp", "expert"), None),
        P("expert", "dp", None),
        P("expert", "dp", None),
        P("expert", None, None),
    )
    return jax.shard_map(shards, mesh=mesh, in_specs=in_specs, out_specs=out_specs, check_vma=False)
```

```python
import functools

import jax
import jax.numpy as jnp
from jax import lax
from jax.experimental import pallas as pl
from jax.experimental.pallas import tpu as pltpu
from jax.sharding import PartitionSpec as P

BASE = 2
SLOTS = 4
MSG = 2 * SLOTS
LANES = 128
CHUNKS = 4
EARLY = 3 * 10**10

F32 = jnp.float32
BF16 = jnp.bfloat16
VMEM = pl.BlockSpec(memory_space=pltpu.VMEM)
ANY = pl.BlockSpec(memory_space=pl.ANY)
SMEM = pl.BlockSpec(memory_space=pltpu.SMEM)
MIB = 1024 * 1024

NN = (((1,), (0,)), ((), ()))
NT = (((1,), (1,)), ((), ()))
TN = (((0,), (0,)), ((), ()))

def dot(a, b, dims):
    return lax.dot_general(a, b, dims, preferred_element_type=F32)

def call(
    body, name, out_shape, in_specs, scratch=(), flops=0, bytes_accessed=0, vmem=16 * MIB, out=VMEM
):
    return pl.pallas_call(
        body,
        name=name,
        out_shape=out_shape,
        in_specs=in_specs,
        out_specs=jax.tree.map(lambda _: out, out_shape),
        scratch_shapes=list(scratch),
        compiler_params=pltpu.CompilerParams(vmem_limit_bytes=vmem),
        cost_estimate=pl.CostEstimate(
            flops=flops, bytes_accessed=bytes_accessed, transcendentals=0
        ),
    )

def identity(n):
    rows = lax.broadcasted_iota(jnp.int32, (n, n), 0)
    return jnp.where(rows == lax.broadcasted_iota(jnp.int32, (n, n), 1), 1.0, 0.0).astype(BF16)

def dispatch_body(
    experts, tok_hbm, cot_hbm, routes_hbm, combine_hbm, hot_hbm, extra_hbm,
    send_hbm, pick_hbm, send, pick_t, both, routes_in, combine_in, hot, extra, sems, out_sems,
):
    count = tok_hbm.shape[0]
    copies = [
        pltpu.make_async_copy(source, target, sems.at[i])
        for i, (source, target) in enumerate(
            [
                (routes_hbm, routes_in),
                (combine_hbm, combine_in),
                (hot_hbm, hot),
                (extra_hbm, extra),
                (tok_hbm, both.at[pl.ds(0, count)]),
                (cot_hbm, both.at[pl.ds(count, count)]),
            ]
        )
    ]
    for copy in copies:
        copy.start()
    for copy in copies[:4]:
        copy.wait()
    lanes = 2 * count
    src = lax.broadcasted_iota(jnp.int32, (count, lanes), 0)
    dst = lax.broadcasted_iota(jnp.int32, (count, lanes), 1)
    dst = jnp.where(dst >= count, dst - count, dst)
    twice = jnp.where(src == dst, 1.0, 0.0).astype(BF16)
    routes = dot(routes_in[...].astype(F32).astype(BF16), twice, NN)
    combine = dot(combine_in[...], twice, NN)
    expert_id = lax.broadcasted_iota(jnp.int32, (experts, lanes), 0)
    lane = lax.broadcasted_iota(jnp.int32, (experts, lanes), 1)
    named = jnp.zeros((experts, lanes), F32)
    weight = jnp.zeros((experts, lanes), F32)
    expert_number = expert_id.astype(F32)
    for k in range(routes.shape[0]):
        match = expert_number == routes[k : k + 1, :]
        named = named + jnp.where(match, 1.0, 0.0)
        weight = weight + jnp.where(match, combine[k : k + 1, :], 0.0)
    before = jnp.where(src < dst, 1.0, 0.0).astype(BF16)
    rank = dot(named[:, :count].astype(BF16), before, NN)
    limit = jnp.full((experts, lanes), float(BASE), F32)
    for j in range(hot.shape[0]):
        limit = limit + jnp.where(expert_id == hot[j], extra[j].astype(F32), 0.0)
    place = jnp.where(lane >= count, rank + float(SLOTS), rank)
    place = jnp.where(named > 0.5, place, -1.0)
    place = jnp.where(rank < limit, place, -1.0)
    weight = jnp.where(lane >= count, weight, 1.0)
    slot = lax.broadcasted_iota(jnp.int32, (experts, MSG, lanes), 1).astype(F32)
    hit = jnp.broadcast_to(place[:, None, :], (experts, MSG, lanes)) == slot
    scaled = jnp.where(hit, jnp.broadcast_to(weight[:, None, :], hit.shape), 0.0)
    scaled = scaled.reshape(experts * MSG, lanes).astype(BF16)
    for copy in copies[4:]:
        copy.wait()
    part = send.shape[0] // CHUNKS
    departures = []
    for n in range(CHUNKS):
        at = pl.ds(n * part, part)
        block = dot(scaled[n * part : (n + 1) * part, :], both[...], NN)
        send[at, :] = block.astype(BF16)
        departures += start_all([pltpu.make_async_copy(send.at[at], send_hbm.at[at], out_sems.at[n])])
    pick = jnp.where(hit, 1.0, 0.0).reshape(experts * MSG, lanes).astype(BF16)
    pick_t[...] = dot(identity(lanes), pick, NT).astype(BF16)
    departures += start_all([pltpu.make_async_copy(pick_t, pick_hbm, out_sems.at[CHUNKS])])
    wait_all(departures)

def token_body(pick_t, returned, out):
    count, half = out.shape[0], returned.shape[1]
    both = dot(pick_t[...], returned[...], NN)
    out[:, :half] = both[:count].astype(BF16)
    out[:, half:] = both[count:].astype(BF16)

def start_all(copies):
    for copy in copies:
        copy.start()
    return copies

def wait_all(copies):
    for copy in copies:
        copy.wait()

def expert_body(
    ranks, me, recv_hbm, w_gate_hbm, w_up_hbm, w_down_hbm,
    back_hbm, down_out_hbm, send_hbm, keep_hbm, back, down_out, send, keep,
    recv, w_in, w_down, wide, narrow, tok, og, pre, grad, in_rows, hid, total, in_sems, out_sems,
):
    rows_in, features = recv.shape
    hidden = w_down.shape[0]
    peers = rows_in // MSG
    half = features // 2
    step = rows_in // CHUNKS
    chunks = [pl.ds(n * step, step) for n in range(CHUNKS)]
    arrivals = start_all(
        [
            pltpu.make_async_copy(recv_hbm.at[at], recv.at[at], in_sems.at[n])
            for n, at in enumerate(chunks)
        ]
    )
    weights = start_all(
        [
            pltpu.make_async_copy(source, target, in_sems.at[CHUNKS + n])
            for n, (source, target) in enumerate(
                [
                    (w_gate_hbm, w_in.at[:, pl.ds(0, hidden)]),
                    (w_up_hbm, w_in.at[:, pl.ds(hidden, hidden)]),
                    (w_down_hbm, w_down),
                ]
            )
        ]
    )
    departures = []

    def send_out(source, target):
        copy = pltpu.make_async_copy(source, target, out_sems.at[len(departures)])
        departures.extend(start_all([copy]))

    for copy, at in zip(arrivals, chunks):
        copy.wait()
        for c in range(features // LANES):
            wide[c, at, :] = recv[at, c * LANES : (c + 1) * LANES].astype(F32)
    for s in range(SLOTS):
        at = pl.ds(s * peers, peers)
        for c in range(features // LANES):
            cols = slice(c * LANES, (c + 1) * LANES)
            tok[at, cols] = wide[c, pl.ds(s, peers, MSG), :].astype(BF16)
            og[at, cols] = wide[c, pl.ds(s + SLOTS, peers, MSG), :].astype(BF16)
    wait_all(weights)
    pre[...] = dot(tok[...], w_in[...], NN)
    grad[...] = dot(og[...], w_down[...], NT)
    for at in range(0, SLOTS * peers, peers):
        rows = slice(at, at + peers)
        gate_pre, up_proj, hidden_grad = pre[rows, :hidden], pre[rows, hidden:], grad[rows, :]
        s = jax.nn.sigmoid(gate_pre)
        act = gate_pre * s
        hid[rows, :] = (act * up_proj).astype(BF16)
        gate_grad = hidden_grad * up_proj * s * (1.0 + gate_pre * (1.0 - s))
        in_rows[rows, :hidden] = gate_grad.astype(BF16)
        in_rows[rows, hidden:] = (hidden_grad * act).astype(BF16)
    grads = dot(in_rows[...], w_in[...], NT)
    for s in range(SLOTS):
        piece = grads[s * peers : (s + 1) * peers, :]
        for c in range(half // LANES):
            low = piece[:, c * LANES : (c + 1) * LANES]
            high = piece[:, half + c * LANES : half + (c + 1) * LANES]
            narrow[c, pl.ds(s, peers, MSG), :] = low
            narrow[c, pl.ds(s + SLOTS, peers, MSG), :] = high
    for c in range(half // LANES):
        back[:, c * LANES : (c + 1) * LANES] = narrow[c].astype(BF16)
    send_out(back, back_hbm)
    total[...] = dot(tok[...], in_rows[...], TN)
    piece = features // ranks
    even = me[0] + 1 - 2 * lax.rem(me[0], 2)

    def part_of(index):
        return total[pl.ds(pl.multiple_of(index * piece, 16), piece), :].astype(BF16)

    send[:, : 2 * hidden] = part_of(ranks - 1 - even)
    send[:, 2 * hidden :] = part_of(even)
    send_out(send, send_hbm)
    keep[:, : 2 * hidden] = part_of(ranks - 1 - me[0])
    keep[:, 2 * hidden :] = part_of(me[0])
    send_out(keep, keep_hbm)
    down_out[...] = dot(hid[...], og[...], TN).astype(BF16)
    send_out(down_out, down_out_hbm)
    wait_all(departures)

def add(kept, received):
    return kept.astype(F32) + received.astype(F32)

def sum_body(kept, received, out):
    width = out.shape[1]
    out[...] = add(kept[:, :width], received[:, :width]).astype(BF16)

def pair_body(keep, first, second, grad_gate, grad_up):
    hidden = grad_gate.shape[1]
    own = add(keep[:, 2 * hidden :], first[:, 2 * hidden :]) + second[...].astype(F32)
    grad_gate[...] = own[:, :hidden].astype(BF16)
    grad_up[...] = own[:, hidden:].astype(BF16)

def shards(tokens, cotangent, routes, combine, hot_experts, extra_slots, w_gate, w_up, w_down):
    experts = lax.axis_size("expert")
    ranks = lax.axis_size("dp")
    count, features = tokens.shape
    hidden = w_gate.shape[2]
    total = experts * MSG
    rows = experts * SLOTS
    me = lax.axis_index("dp").astype(jnp.int32).reshape(1)
    me, hot_experts = lax.optimization_barrier((me, hot_experts))
    send, pick_t = call(
        functools.partial(dispatch_body, experts),
        "dispatch",
        [
            jax.ShapeDtypeStruct((total, features), BF16),
            jax.ShapeDtypeStruct((2 * count, total), BF16),
        ],
        [ANY] * 6,
        [
            pltpu.VMEM((total, features), BF16),
            pltpu.VMEM((2 * count, total), BF16),
            pltpu.VMEM((2 * count, features), BF16),
            pltpu.VMEM(routes.shape[::-1], jnp.int32),
            pltpu.VMEM(combine.shape[::-1], BF16),
            pltpu.SMEM(hot_experts.shape, jnp.int32),
            pltpu.SMEM(extra_slots.shape, jnp.int32),
            pltpu.SemaphoreType.DMA((6,)),
            pltpu.SemaphoreType.DMA((CHUNKS + 1,)),
        ],
        2 * total * 2 * count * features,
        2 * total * features,
        64 * MIB - 65536,
        ANY,
    )(tokens, cotangent, routes.T, combine.T, hot_experts, extra_slots)
    recv = lax.all_to_all(send, "expert", split_axis=0, concat_axis=0, tiled=True)
    piece = features // ranks
    shape = jax.ShapeDtypeStruct
    out = [shape((total, features // 2), BF16)]
    whole_down = shape((hidden, features), BF16)
    out += [whole_down] + [shape((piece, 4 * hidden), BF16)] * 2
    back, down, send, keep = call(
        functools.partial(expert_body, ranks),
        "expert",
        out,
        [SMEM] + [ANY] * 4,
        [pltpu.VMEM(a.shape, a.dtype) for a in out]
        + [
            pltpu.VMEM((total, features), BF16),
            pltpu.VMEM((features, 2 * hidden), BF16),
            pltpu.VMEM((hidden, features), BF16),
            pltpu.VMEM((features // LANES, total, LANES), F32),
            pltpu.VMEM((features // 2 // LANES, total, LANES), F32),
            pltpu.VMEM((rows, features), BF16),
            pltpu.VMEM((rows, features), BF16),
            pltpu.VMEM((rows, 2 * hidden), F32),
            pltpu.VMEM((rows, hidden), F32),
            pltpu.VMEM((rows, 2 * hidden), BF16),
            pltpu.VMEM((rows, hidden), BF16),
            pltpu.VMEM((features, 2 * hidden), F32),
            pltpu.SemaphoreType.DMA((CHUNKS + 3,)),
            pltpu.SemaphoreType.DMA((len(out),)),
        ],
        16 * rows * features * hidden,
        2 * (total * features * 2 + 6 * features * hidden),
        44 * MIB,
        ANY,
    )(me, recv, w_gate[0], w_up[0], w_down[0])
    returned = lax.all_to_all(back, "expert", split_axis=0, concat_axis=0, tiled=True)

    def even(value):
        return lax.ppermute(value, "dp", [(i, i ^ 1) for i in range(ranks)])

    def mirror(value):
        return lax.ppermute(value, "dp", [(i, ranks - 1 - i) for i in range(ranks)])

    def small(body, name, out, *operands, work=0):
        moved = sum(2 * a.size for a in operands) + sum(2 * a.size for a in jax.tree.leaves(out))
        return call(
            body, name, out, [VMEM] * len(operands), flops=work, bytes_accessed=moved
        )(*operands)

    one_piece = shape((piece, hidden), BF16)
    first = even(send)
    first_down = mirror(down)
    both_pieces = shape((piece, 2 * hidden), BF16)
    sum_down = small(sum_body, "down_sum", whole_down, down, first_down)
    next_down = even(sum_down)
    pair_sum = small(sum_body, "pair_sum", both_pieces, keep, first, work=EARLY)
    second = mirror(pair_sum)
    grad_down = small(sum_body, "down", whole_down, sum_down, next_down)
    grad_gate, grad_up = small(pair_body, "pair", [one_piece, one_piece], keep, first, second)
    token_grads = call(
        token_body,
        "token_grad",
        jax.ShapeDtypeStruct((count, features), BF16),
        [VMEM, VMEM],
        (),
        2 * total * count * features,
        2 * total * features,
    )(pick_t, returned)
    return token_grads, grad_gate[None], grad_up[None], grad_down[None]

def solution(mesh):
    in_specs = (
        P(("dp", "expert"), None),
        P(("dp", "expert"), None),
        P(("dp", "expert"), None),
        P(("dp", "expert"), None),
        P(),
        P(),
        P("expert", None, None),
        P("expert", None, None),
        P("expert", None, None),
    )
    out_specs = (
        P(("dp", "expert"), None),
        P("expert", "dp", None),
        P("expert", "dp", None),
        P("expert", None, None),
    )
    return jax.shard_map(shards, mesh=mesh, in_specs=in_specs, out_specs=out_specs, check_vma=False)
```

```python
import functools

import jax
import jax.numpy as jnp
from jax import lax
from jax.experimental import pallas as pl
from jax.experimental.pallas import tpu as pltpu
from jax.sharding import PartitionSpec as P

BASE = 2
SLOTS = 4
MSG = 2 * SLOTS
LANES = 128
CHUNKS = 4
EARLY = 3 * 10**10

F32 = jnp.float32
BF16 = jnp.bfloat16
VMEM = pl.BlockSpec(memory_space=pltpu.VMEM)
ANY = pl.BlockSpec(memory_space=pl.ANY)
SMEM = pl.BlockSpec(memory_space=pltpu.SMEM)
MIB = 1024 * 1024

NN = (((1,), (0,)), ((), ()))
NT = (((1,), (1,)), ((), ()))
TN = (((0,), (0,)), ((), ()))

def dot(a, b, dims):
    return lax.dot_general(a, b, dims, preferred_element_type=F32)

def call(
    body, name, out_shape, in_specs, scratch=(), flops=0, bytes_accessed=0, vmem=16 * MIB, out=VMEM
):
    return pl.pallas_call(
        body,
        name=name,
        out_shape=out_shape,
        in_specs=in_specs,
        out_specs=out if isinstance(out, list) else jax.tree.map(lambda _: out, out_shape),
        scratch_shapes=list(scratch),
        compiler_params=pltpu.CompilerParams(vmem_limit_bytes=vmem),
        cost_estimate=pl.CostEstimate(
            flops=flops, bytes_accessed=bytes_accessed, transcendentals=0
        ),
    )

def identity(n):
    rows = lax.broadcasted_iota(jnp.int32, (n, n), 0)
    return jnp.where(rows == lax.broadcasted_iota(jnp.int32, (n, n), 1), 1.0, 0.0).astype(BF16)

def dispatch_body(
    experts, tok_hbm, cot_hbm, routes_hbm, combine_hbm, hot_hbm, extra_hbm,
    send_hbm, pick_hbm, send, pick_t, both, routes_in, combine_in, hot, extra, sems, out_sems,
):
    count = tok_hbm.shape[0]
    copies = [
        pltpu.make_async_copy(source, target, sems.at[i])
        for i, (source, target) in enumerate(
            [
                (routes_hbm, routes_in),
                (combine_hbm, combine_in),
                (hot_hbm, hot),
                (extra_hbm, extra),
                (tok_hbm, both.at[pl.ds(0, count)]),
                (cot_hbm, both.at[pl.ds(count, count)]),
            ]
        )
    ]
    for copy in copies:
        copy.start()
    for copy in copies[:4]:
        copy.wait()
    lanes = 2 * count
    src = lax.broadcasted_iota(jnp.int32, (count, lanes), 0)
    dst = lax.broadcasted_iota(jnp.int32, (count, lanes), 1)
    dst = jnp.where(dst >= count, dst - count, dst)
    twice = jnp.where(src == dst, 1.0, 0.0).astype(BF16)
    routes = dot(routes_in[...].astype(F32).astype(BF16), twice, NN)
    combine = dot(combine_in[...], twice, NN)
    expert_id = lax.broadcasted_iota(jnp.int32, (experts, lanes), 0)
    lane = lax.broadcasted_iota(jnp.int32, (experts, lanes), 1)
    named = jnp.zeros((experts, lanes), F32)
    weight = jnp.zeros((experts, lanes), F32)
    expert_number = expert_id.astype(F32)
    for k in range(routes.shape[0]):
        match = expert_number == routes[k : k + 1, :]
        named = named + jnp.where(match, 1.0, 0.0)
        weight = weight + jnp.where(match, combine[k : k + 1, :], 0.0)
    before = jnp.where(src < dst, 1.0, 0.0).astype(BF16)
    rank = dot(named[:, :count].astype(BF16), before, NN)
    limit = jnp.full((experts, lanes), float(BASE), F32)
    for j in range(hot.shape[0]):
        limit = limit + jnp.where(expert_id == hot[j], extra[j].astype(F32), 0.0)
    place = jnp.where(lane >= count, rank + float(SLOTS), rank)
    place = jnp.where(named > 0.5, place, -1.0)
    place = jnp.where(rank < limit, place, -1.0)
    weight = jnp.where(lane >= count, weight, 1.0)
    slot = lax.broadcasted_iota(jnp.int32, (experts, MSG, lanes), 1).astype(F32)
    hit = jnp.broadcast_to(place[:, None, :], (experts, MSG, lanes)) == slot
    scaled = jnp.where(hit, jnp.broadcast_to(weight[:, None, :], hit.shape), 0.0)
    scaled = scaled.reshape(experts * MSG, lanes).astype(BF16)
    pick = jnp.where(hit, 1.0, 0.0).reshape(experts * MSG, lanes).astype(BF16)
    pick_t[...] = dot(identity(lanes), pick, NT).astype(BF16)
    departures = start_all([pltpu.make_async_copy(pick_t, pick_hbm, out_sems.at[CHUNKS])])
    for copy in copies[4:]:
        copy.wait()
    part = send.shape[0] // CHUNKS
    for n in range(CHUNKS):
        at = pl.ds(n * part, part)
        block = dot(scaled[n * part : (n + 1) * part, :], both[...], NN)
        send[at, :] = block.astype(BF16)
        departures += start_all([pltpu.make_async_copy(send.at[at], send_hbm.at[at], out_sems.at[n])])
    wait_all(departures)

def token_body(pick_t, returned, out):
    count, half = out.shape[0], returned.shape[1]
    both = dot(pick_t[...], returned[...], NN)
    out[:, :half] = both[:count].astype(BF16)
    out[:, half:] = both[count:].astype(BF16)

def start_all(copies):
    for copy in copies:
        copy.start()
    return copies

def wait_all(copies):
    for copy in copies:
        copy.wait()

def expert_body(
    ranks, me, recv, w_gate_hbm, w_up_hbm, w_down_hbm,
    back_hbm, down_out, send, keep, back,
    w_in, w_down, wide, narrow, tok, og, pre, grad, in_rows, hid, total, in_sems, out_sem,
):
    rows_in, features = recv.shape
    hidden = w_down.shape[0]
    peers = rows_in // MSG
    half = features // 2
    weights = start_all(
        [
            pltpu.make_async_copy(source, target, in_sems.at[n])
            for n, (source, target) in enumerate(
                [
                    (w_gate_hbm, w_in.at[:, pl.ds(0, hidden)]),
                    (w_up_hbm, w_in.at[:, pl.ds(hidden, hidden)]),
                    (w_down_hbm, w_down),
                ]
            )
        ]
    )
    for c in range(features // LANES):
        wide[c] = recv[:, c * LANES : (c + 1) * LANES].astype(F32)
    for s in range(SLOTS):
        at = pl.ds(s * peers, peers)
        for c in range(features // LANES):
            cols = slice(c * LANES, (c + 1) * LANES)
            tok[at, cols] = wide[c, pl.ds(s, peers, MSG), :].astype(BF16)
            og[at, cols] = wide[c, pl.ds(s + SLOTS, peers, MSG), :].astype(BF16)
    wait_all(weights)
    pre[...] = dot(tok[...], w_in[...], NN)
    grad[...] = dot(og[...], w_down[...], NT)
    for at in range(0, SLOTS * peers, peers):
        rows = slice(at, at + peers)
        gate_pre, up_proj, hidden_grad = pre[rows, :hidden], pre[rows, hidden:], grad[rows, :]
        s = jax.nn.sigmoid(gate_pre)
        act = gate_pre * s
        hid[rows, :] = (act * up_proj).astype(BF16)
        gate_grad = hidden_grad * up_proj * s * (1.0 + gate_pre * (1.0 - s))
        in_rows[rows, :hidden] = gate_grad.astype(BF16)
        in_rows[rows, hidden:] = (hidden_grad * act).astype(BF16)
    grads = dot(in_rows[...], w_in[...], NT)
    for s in range(SLOTS):
        piece = grads[s * peers : (s + 1) * peers, :]
        for c in range(half // LANES):
            low = piece[:, c * LANES : (c + 1) * LANES]
            high = piece[:, half + c * LANES : half + (c + 1) * LANES]
            narrow[c, pl.ds(s, peers, MSG), :] = low
            narrow[c, pl.ds(s + SLOTS, peers, MSG), :] = high
    for c in range(half // LANES):
        back[:, c * LANES : (c + 1) * LANES] = narrow[c].astype(BF16)
    departures = start_all([pltpu.make_async_copy(back, back_hbm, out_sem)])
    total[...] = dot(tok[...], in_rows[...], TN)
    piece = features // ranks
    even = me[0] + 1 - 2 * lax.rem(me[0], 2)

    def part_of(index):
        return total[pl.ds(pl.multiple_of(index * piece, 16), piece), :].astype(BF16)

    send[:, : 2 * hidden] = part_of(ranks - 1 - even)
    send[:, 2 * hidden :] = part_of(even)
    keep[:, : 2 * hidden] = part_of(ranks - 1 - me[0])
    keep[:, 2 * hidden :] = part_of(me[0])
    down_out[...] = dot(hid[...], og[...], TN).astype(BF16)
    wait_all(departures)

def add(kept, received):
    return kept.astype(F32) + received.astype(F32)

def sum_body(kept, received, out):
    width = out.shape[1]
    out[...] = add(kept[:, :width], received[:, :width]).astype(BF16)

def pair_body(keep, first, second, grad_gate, grad_up):
    hidden = grad_gate.shape[1]
    own = add(keep[:, 2 * hidden :], first[:, 2 * hidden :]) + second[...].astype(F32)
    grad_gate[...] = own[:, :hidden].astype(BF16)
    grad_up[...] = own[:, hidden:].astype(BF16)

def shards(tokens, cotangent, routes, combine, hot_experts, extra_slots, w_gate, w_up, w_down):
    experts = lax.axis_size("expert")
    ranks = lax.axis_size("dp")
    count, features = tokens.shape
    hidden = w_gate.shape[2]
    total = experts * MSG
    rows = experts * SLOTS
    me = lax.axis_index("dp").astype(jnp.int32).reshape(1)
    me, hot_experts = lax.optimization_barrier((me, hot_experts))
    send, pick_t = call(
        functools.partial(dispatch_body, experts),
        "dispatch",
        [
            jax.ShapeDtypeStruct((total, features), BF16),
            jax.ShapeDtypeStruct((2 * count, total), BF16),
        ],
        [ANY] * 6,
        [
            pltpu.VMEM((total, features), BF16),
            pltpu.VMEM((2 * count, total), BF16),
            pltpu.VMEM((2 * count, features), BF16),
            pltpu.VMEM(routes.shape[::-1], jnp.int32),
            pltpu.VMEM(combine.shape[::-1], BF16),
            pltpu.SMEM(hot_experts.shape, jnp.int32),
            pltpu.SMEM(extra_slots.shape, jnp.int32),
            pltpu.SemaphoreType.DMA((6,)),
            pltpu.SemaphoreType.DMA((CHUNKS + 1,)),
        ],
        2 * total * 2 * count * features,
        2 * total * features,
        64 * MIB - 65536,
        ANY,
    )(tokens, cotangent, routes.T, combine.T, hot_experts, extra_slots)
    recv = lax.all_to_all(send, "expert", split_axis=0, concat_axis=0, tiled=True)
    piece = features // ranks
    shape = jax.ShapeDtypeStruct
    out = [shape((total, features // 2), BF16)]
    whole_down = shape((hidden, features), BF16)
    out += [whole_down] + [shape((piece, 4 * hidden), BF16)] * 2
    back, down, send, keep = call(
        functools.partial(expert_body, ranks),
        "expert",
        out,
        [SMEM, VMEM] + [ANY] * 3,
        [pltpu.VMEM(out[0].shape, BF16)]
        + [
            pltpu.VMEM((features, 2 * hidden), BF16),
            pltpu.VMEM((hidden, features), BF16),
            pltpu.VMEM((features // LANES, total, LANES), F32),
            pltpu.VMEM((features // 2 // LANES, total, LANES), F32),
            pltpu.VMEM((rows, features), BF16),
            pltpu.VMEM((rows, features), BF16),
            pltpu.VMEM((rows, 2 * hidden), F32),
            pltpu.VMEM((rows, hidden), F32),
            pltpu.VMEM((rows, 2 * hidden), BF16),
            pltpu.VMEM((rows, hidden), BF16),
            pltpu.VMEM((features, 2 * hidden), F32),
            pltpu.SemaphoreType.DMA((3,)),
            pltpu.SemaphoreType.DMA(()),
        ],
        16 * rows * features * hidden,
        2 * (total * features * 2 + 6 * features * hidden),
        44 * MIB,
        [ANY] + [VMEM] * 3,
    )(me, recv, w_gate[0], w_up[0], w_down[0])
    returned = lax.all_to_all(back, "expert", split_axis=0, concat_axis=0, tiled=True)

    def even(value):
        return lax.ppermute(value, "dp", [(i, i ^ 1) for i in range(ranks)])

    def mirror(value):
        return lax.ppermute(value, "dp", [(i, ranks - 1 - i) for i in range(ranks)])

    def small(body, name, out, *operands, work=0):
        moved = sum(2 * a.size for a in operands) + sum(2 * a.size for a in jax.tree.leaves(out))
        return call(
            body, name, out, [VMEM] * len(operands), flops=work, bytes_accessed=moved
        )(*operands)

    one_piece = shape((piece, hidden), BF16)
    first = even(send)
    first_down = mirror(down)
    both_pieces = shape((piece, 2 * hidden), BF16)
    sum_down = small(sum_body, "down_sum", whole_down, down, first_down)
    next_down = even(sum_down)
    pair_sum = small(sum_body, "pair_sum", both_pieces, keep, first, work=EARLY)
    second = mirror(pair_sum)
    grad_down = small(sum_body, "down", whole_down, sum_down, next_down)
    grad_gate, grad_up = small(pair_body, "pair", [one_piece, one_piece], keep, first, second)
    token_grads = call(
        token_body,
        "token_grad",
        jax.ShapeDtypeStruct((count, features), BF16),
        [VMEM, VMEM],
        (),
        2 * total * count * features,
        2 * total * features,
    )(pick_t, returned)
    return token_grads, grad_gate[None], grad_up[None], grad_down[None]

def solution(mesh):
    in_specs = (
        P(("dp", "expert"), None),
        P(("dp", "expert"), None),
        P(("dp", "expert"), None),
        P(("dp", "expert"), None),
        P(),
        P(),
        P("expert", None, None),
        P("expert", None, None),
        P("expert", None, None),
    )
    out_specs = (
        P(("dp", "expert"), None),
        P("expert", "dp", None),
        P("expert", "dp", None),
        P("expert", None, None),
    )
    return jax.shard_map(shards, mesh=mesh, in_specs=in_specs, out_specs=out_specs, check_vma=False)
```
